512 devices in a mesh: rows: 128 (over z, x_lo, y), batch: 4 (over x_hi, core).
Axes of the slice: x: 4 (x_hi: 2, x_lo: 2; x = x_hi * 2 + x_lo), y: 4, z: 16, core: 2. Of those that a mesh axis runs over, the one named last changes fastest.
Arguments:
- hidden_states: bfloat16 [16384, 1280], P(('batch', 'rows')), parts along dimension 0, may hold values from -1000 to 1000
- norm_gain: float32 [1280], replicated, may hold values from 0.1 to 1.9
- norm_bias: float32 [1280], replicated, may hold values from -3 to 3
- query_weight: bfloat16 [1280, 640], replicated, may hold values from -0.15625 to 0.15625
- key_weight: bfloat16 [1280, 640], replicated, may hold values from -0.15625 to 0.15625
- value_weight: bfloat16 [1280, 640], replicated, may hold values from -0.15625 to 0.15625
- stale_keys: bfloat16 [16384, 640], P(('batch', 'rows')), parts along dimension 0, may hold values from -370 to 370
- stale_values: bfloat16 [16384, 640], P(('batch', 'rows')), parts along dimension 0, may hold values from -6 to 6
Outputs:
- attention: bfloat16 [16384, 640], P(('batch', 'rows')), parts along dimension 0
- fresh_keys: bfloat16 [16384, 640], P(('batch', 'rows')), parts along dimension 0
- fresh_values: bfloat16 [16384, 640], P(('batch', 'rows')), parts along dimension 0
The draws below stay inside these ranges and needn't reach their ends.
There are 4 independent parts, one for each index of `batch`. The reference program is written for one: setup_inputs(seed, part) draws one part's arguments, and reference() takes and returns one part's arrays. A program takes and returns all parts, laid end to end along the dimension named above; an argument that names none is the same for every part. Nothing has to cross between parts.
All inputs are finite; a program needn't handle non-finite values.
Results may differ from the reference program's by a relative error of at most 0.013.
The reference program's roundings to bfloat16 on the way count: a program that leaves them out, or rounds other values in their place, can miss the bound.
Values may be sent and summed in bfloat16 or wider, within the bound.
A program may use at most 64 MiB of HBM per device.

```python
import jax
import jax.numpy as jnp
from jax import lax

CHANNELS = 1280
GROUPS = 32
HEADS = 10
HEAD_DIM = 64
TOK_DEV = 32
TOKENS = 4096
ATTN_WIDTH = 640
N_ROWS = 128


def draw_hidden_states(key, part):
    key = jax.random.fold_in(key, 11)
    base_key, row_key, col_key, shift_key = jax.random.split(key, 4)
    positions = jnp.arange(TOKENS, dtype=jnp.float32) / max(TOKENS - 1, 1)
    base = jax.random.truncated_normal(base_key, -4.0, 4.0, (TOKENS, CHANNELS), jnp.float32)
    rising = 1.0 + 2.0 * positions
    row_scale = jnp.exp(jax.random.uniform(row_key, (TOKENS,), jnp.float32, jnp.log(0.3), jnp.log(3.0)))
    col_scale = jnp.exp(jax.random.uniform(col_key, (CHANNELS,), jnp.float32, 0.0, jnp.log(10.0)))
    offsets = 0.5 * jax.random.truncated_normal(shift_key, -4.0, 4.0, (CHANNELS,), jnp.float32)
    result = (base + offsets[None, :]) * col_scale[None, :] * (row_scale * rising)[:, None]
    return result.astype(jnp.bfloat16)


def draw_stale_keys(key, part):
    key = jax.random.fold_in(key, 23)
    base = jax.random.truncated_normal(key, -4.0, 4.0, (TOKENS, ATTN_WIDTH), jnp.float32)
    return base.astype(jnp.bfloat16)


def steps_of(stream_key, extent, cuts, smallest, high):
    gain, own = 1.0, jax.random.fold_in(stream_key, 6)
    for position, blocks in cuts:
        heights = jnp.exp(jax.random.uniform(jax.random.fold_in(own, position), (blocks,), jnp.float32, smallest / len(cuts), high / len(cuts)))
        gain = gain * jnp.repeat(heights, extent[position] // blocks).reshape([-1 if axis == position else 1 for axis in range(len(extent))])
    return gain


def normal_values(stream_key, dims, width, bound, shards=(), kind=jnp.bfloat16):
    gain = steps_of(stream_key, dims, shards, -0.22, 0.18) if shards else 1.0
    values = jax.random.normal(stream_key, dims, jnp.float32) * width * gain
    return jnp.minimum(jnp.maximum(values, -bound), bound).astype(kind)


def setup_inputs(seed: int = 0, part: int = 0) -> dict:
    seeds = jax.random.split(jax.random.key(seed), 9)
    part_splits = jax.random.split(jax.random.fold_in(seeds[8], part), 9)
    hidden_states = draw_hidden_states(jax.random.fold_in(jax.random.fold_in(seeds[8], part), 71), part)
    norm_gain = jnp.clip(1.0 + 0.18 * jax.random.normal(seeds[1], (CHANNELS,), jnp.float32), 0.1, 1.9)
    norm_bias = normal_values(seeds[2], (CHANNELS,), 0.5, 3.0, (), jnp.float32)
    query_weight = normal_values(seeds[3], (CHANNELS, ATTN_WIDTH), CHANNELS ** -0.5, 0.15625)
    key_weight = normal_values(seeds[4], (CHANNELS, ATTN_WIDTH), CHANNELS ** -0.5, 0.15625)
    value_weight = normal_values(seeds[5], (CHANNELS, ATTN_WIDTH), CHANNELS ** -0.5, 0.15625)
    stale_keys = draw_stale_keys(jax.random.fold_in(jax.random.fold_in(seeds[8], part), 71), part)
    stale_values = normal_values(part_splits[7], (TOKENS, ATTN_WIDTH), 1.0, 6.0, ((0, 128),))
    return {"hidden_states": hidden_states, "norm_gain": norm_gain, "norm_bias": norm_bias, "query_weight": query_weight, "key_weight": key_weight, "value_weight": value_weight, "stale_keys": stale_keys, "stale_values": stale_values}


def group_average(channel_totals, count):
    grouped = channel_totals.reshape(GROUPS, -1).sum(axis=1) / count
    return jnp.repeat(grouped, channel_totals.shape[0] // GROUPS)

def attend(query, key_rows, value_rows):
    scaling = HEAD_DIM ** (-0.5)
    keys_three = key_rows.reshape(-1, HEADS, HEAD_DIM).astype(jnp.float32)
    values_three = value_rows.reshape(-1, HEADS, HEAD_DIM).astype(jnp.float32)
    scores = jnp.einsum('qhd,khd->qhk', query.astype(jnp.float32), keys_three) * scaling
    largest = lax.optimization_barrier(jnp.max(scores, axis=-1))
    unrounded = jnp.exp(scores - largest[..., None])
    totals = lax.optimization_barrier(jnp.sum(unrounded, axis=-1))
    rounded = lax.optimization_barrier(unrounded.astype(jnp.bfloat16)).astype(jnp.float32)
    weighted = jnp.einsum('qhk,khd->qhd', rounded, values_three)
    return weighted / totals[..., None]

def reference(hidden_states, norm_gain, norm_bias, query_weight, key_weight, value_weight, stale_keys, stale_values):
    widened = hidden_states.astype(jnp.float32)
    group_count = TOKENS * (CHANNELS // GROUPS)
    mean_chan = group_average(lax.optimization_barrier(jnp.sum(widened, axis=0)), group_count)
    centered = widened - mean_chan
    var_chan = group_average(lax.optimization_barrier(jnp.sum(centered * centered, axis=0)), group_count)
    normed = (centered * lax.rsqrt(var_chan + 1e-05) * norm_gain + norm_bias).astype(jnp.bfloat16)
    query_all = jnp.dot(normed, query_weight, preferred_element_type=jnp.float32).astype(jnp.bfloat16)
    fresh_keys = jnp.dot(normed, key_weight, preferred_element_type=jnp.float32).astype(jnp.bfloat16)
    fresh_values = jnp.dot(normed, value_weight, preferred_element_type=jnp.float32).astype(jnp.bfloat16)

    def one_block(index):
        start = (index * TOK_DEV).astype(jnp.int32)
        zero = jnp.int32(0)
        query = lax.dynamic_slice_in_dim(query_all, start, TOK_DEV, 0).reshape(TOK_DEV, HEADS, HEAD_DIM)
        key_rows = lax.dynamic_update_slice(stale_keys, lax.dynamic_slice_in_dim(fresh_keys, start, TOK_DEV, 0), (start, zero))
        value_rows = lax.dynamic_update_slice(stale_values, lax.dynamic_slice_in_dim(fresh_values, start, TOK_DEV, 0), (start, zero))
        return attend(query, key_rows, value_rows)
    blocks = lax.map(one_block, jnp.arange(N_ROWS, dtype=jnp.int32))
    attention = blocks.reshape(TOKENS, ATTN_WIDTH).astype(jnp.bfloat16)
    return (attention, fresh_keys, fresh_values)
```

```python
import functools

import jax
import jax.numpy as jnp
from jax import lax
from jax.experimental import pallas as pl
from jax.experimental.pallas import tpu as pltpu
from jax.sharding import PartitionSpec as P

CHANNELS = 1280
GROUPS = 32
GROUP_WIDTH = CHANNELS // GROUPS
HEADS = 10
HEAD_DIM = 64
WIDTH = HEADS * HEAD_DIM
PAIRS = HEADS // 2
EPSILON = 1e-05
PLANE = 8

F32 = jnp.float32
BF16 = jnp.bfloat16
MESH = pl.DeviceIdType.MESH
NT = (((1,), (1,)), ((), ()))


def exact_dot(value, right, dims):
    first = value.astype(BF16).astype(F32)
    second = (value - first).astype(BF16).astype(F32)
    terms = jnp.concatenate([first, second, value - first - second], axis=0).astype(BF16)
    out = lax.dot_general(terms, right, dims, preferred_element_type=F32)
    return out[0:8] + out[8:16] + out[16:24]


def to_groups(value, member):
    return exact_dot(value, member, (((1,), (0,)), ((), ())))


def to_channels(value, member):
    return exact_dot(value, member, NT)


def kernel(
    depth, plane, tokens,
    x_in, gain, bias, wq_in, wk_in, wv_in, k_in, v_in,
    result,
    x_own, kbuf, vbuf, wq, wk, wv, member, qbuf, st1, st2,
    part_o, part_m, part_l, obuf, rbuf, ostat, ostat_packed, rstat_packed,
    in_sem, s1_send, s1_recv, s2_send, s2_recv, q_send, q_recv,
    k_send, k_recv, v_send, v_recv, o_send, o_recv, t_send, t_recv,
):
    row = lax.axis_index("rows")
    z, p = row // plane, lax.rem(row, plane)
    half = depth // 2

    def in_plane(step):
        return {"rows": z * plane + lax.rem(p + step, plane)}

    def in_depth(step):
        return {"rows": lax.rem(z + step, depth) * plane + p}

    def remote(src, dst, send, recv, device):
        return pltpu.make_async_remote_copy(
            src_ref=src, dst_ref=dst, send_sem=send, recv_sem=recv,
            device_id=device, device_id_type=MESH,
        )

    barrier = pltpu.get_barrier_semaphore()

    @pl.loop(1, depth)
    def _(step):
        pl.semaphore_signal(barrier, inc=1, device_id=in_depth(step), device_id_type=MESH)

    @pl.loop(1, plane)
    def _(step):
        pl.semaphore_signal(barrier, inc=1, device_id=in_plane(step), device_id_type=MESH)

    loads = [
        pltpu.make_async_copy(src, dst, in_sem.at[i])
        for i, (src, dst) in enumerate(
            [(x_in, x_own), (k_in, kbuf.at[0]), (v_in, vbuf.at[0]),
             (wq_in, wq), (wk_in, wk), (wv_in, wv)]
        )
    ]
    for load in loads:
        load.start()

    channel = lax.broadcasted_iota(jnp.int32, (CHANNELS, 128), 0)
    group = lax.broadcasted_iota(jnp.int32, (CHANNELS, 128), 1)
    first = group * GROUP_WIDTH
    inside = (channel >= first) & (channel < first + GROUP_WIDTH) & (group < GROUPS)
    member[...] = jnp.where(inside, 1.0, 0.0).astype(BF16)

    loads[0].wait()
    x = x_own[...]
    count = tokens * GROUP_WIDTH
    mean = jnp.sum(jnp.dot(x, member[...], preferred_element_type=F32), axis=0, keepdims=True) / count
    centered = x.astype(F32) - to_channels(jnp.broadcast_to(mean, (8, 128)), member[...])[0:1]
    squares = jnp.sum((centered * centered).reshape(tokens // 8, 8, CHANNELS), axis=0)
    var = jnp.sum(to_groups(squares, member[...]), axis=0, keepdims=True) / count
    st1[0, 0:1, :] = mean
    st1[0, 1:2, :] = var
    loads[1].wait()
    loads[2].wait()

    pl.semaphore_wait(barrier, plane + depth - 2)

    def stat1(step):
        return remote(st1.at[0], st1.at[step], s1_send.at[step], s1_recv.at[step], in_plane(step))

    def stat2(step):
        return remote(st2.at[0], st2.at[step], s2_send.at[step], s2_recv.at[step], in_depth(step))

    def share(pair, step):
        return remote(
            qbuf.at[pair, 0], qbuf.at[pair, step], q_send.at[pair, step], q_recv.at[pair, step],
            in_plane(step),
        )

    order = [0]
    for step in range(1, half):
        order += [step, depth - step]
    order += [half]
    middle = half
    place = {block: at if at < middle else at + 1 for at, block in enumerate(order)}

    def hop(buf, send, recv, way, step):
        if way == 0:
            ends, device = (step, step + 1), in_depth(1)
        else:
            ends, device = ((depth - step) % depth, depth - step - 1), in_depth(depth - 1)
        here, there = place[ends[0]], place[ends[1]]
        return remote(buf.at[here], buf.at[there], send.at[way, step], recv.at[there], device)

    chains = [
        (kbuf, k_send, k_recv, 0, half),
        (vbuf, v_send, v_recv, 1, half),
        (kbuf, k_send, k_recv, 1, half - 1),
        (vbuf, v_send, v_recv, 0, half - 1),
    ]

    def ring(step):
        for buf, send, recv, way, length in chains:
            if step <= length:
                if step > 0:
                    hop(buf, send, recv, way, step - 1).wait_recv()
                if step < length:
                    hop(buf, send, recv, way, step).start()

    def rings(first, last):
        for step in range(first, min(last, half) + 1):
            ring(step)

    def merged(stats):
        means, spread = stats[:, 0, :], stats[:, 1, :]
        mean = jnp.mean(means, axis=0, keepdims=True)
        apart = means - mean
        return mean, jnp.mean(spread + apart * apart, axis=0, keepdims=True)

    @pl.loop(1, plane)
    def _(step):
        stat1(step).start()

    rings(0, 0)

    @pl.loop(1, plane)
    def _(step):
        stat1(step).wait_recv()

    mean, var = merged(st1[...])
    st2[0, 0:1, :] = mean
    st2[0, 1:2, :] = var

    @pl.loop(1, depth)
    def _(step):
        stat2(step).start()

    rings(1, 1)

    @pl.loop(1, depth)
    def _(step):
        stat2(step).wait_recv()

    mean, var = merged(st2[...])
    line = lax.broadcasted_iota(jnp.int32, (8, 128), 0)
    wide = to_channels(jnp.where(line == 0, mean, lax.rsqrt(var + EPSILON)), member[...])
    mean_chan = wide[0:1]
    scale_chan = wide[1:2] * gain[...].reshape(1, CHANNELS)
    bias_chan = bias[...].reshape(1, CHANNELS)
    normed = ((x_own[...].astype(F32) - mean_chan) * scale_chan + bias_chan).astype(BF16)

    rings(2, 2)
    loads[3].wait()
    query = jnp.dot(normed, wq[...], preferred_element_type=F32).astype(BF16)
    query = query * jnp.asarray(HEAD_DIM**-0.5, BF16)
    for pair in range(PAIRS):
        qbuf[pair, 0] = query[:, pair * 128 : (pair + 1) * 128]

    @pl.loop(0, PAIRS)
    def _(pair):
        @pl.loop(1, plane)
        def _(step):
            share(pair, step).start()

    rings(3, 3)
    loads[4].wait()
    fresh = jnp.dot(normed, wk[...], preferred_element_type=F32).astype(BF16)
    kbuf[middle] = fresh
    result[1] = fresh
    rings(4, 4)
    loads[5].wait()
    fresh = jnp.dot(normed, wv[...], preferred_element_type=F32).astype(BF16)
    vbuf[middle] = fresh
    result[2] = fresh

    lane = lax.broadcasted_iota(jnp.int32, (1, 128), 1)
    low = lane < HEAD_DIM
    masks = (jnp.where(low, 1.0, 0.0).astype(BF16), jnp.where(low, 0.0, 1.0).astype(BF16))
    keys_len = half * tokens
    ones = jnp.ones((keys_len, 128), BF16)

    def attend(query, start, pair):
        cols = pl.ds(pl.multiple_of(pair * 128, 128), 128)
        keys = kbuf[start : start + half, :, cols].reshape(keys_len, 128)
        values = vbuf[start : start + half, :, cols].reshape(keys_len, 128)
        count = query.shape[0]
        both = jnp.concatenate([query * masks[0], query * masks[1]], axis=0)
        scores = lax.dot_general(both, keys, NT, preferred_element_type=F32)
        largest = jnp.max(scores, axis=-1, keepdims=True)
        exps = jnp.exp(scores - largest).astype(BF16)
        sums = jnp.dot(exps, jnp.concatenate([values, ones], axis=1), preferred_element_type=F32)

        def pick(tall):
            return jnp.where(low, tall[0:count], tall[count:])

        return pick(sums[:, 0:128]), pick(jnp.broadcast_to(largest, (2 * count, 128))), pick(sums[:, 128:])

    def keep(pair, first, last, parts):
        for buf, value in zip((part_o, part_m, part_l), parts):
            buf[pair, first:last] = value

    rows = plane * tokens

    @pl.loop(0, PAIRS)
    def _(pair):
        keep(pair, 0, tokens, attend(qbuf[pair, 0], 1, pair))

    rings(5, 6)

    def first_half(pair):
        @pl.loop(1, plane)
        def _(step):
            share(pair, step).wait_recv()

        others = qbuf[pair, 1:plane].reshape(rows - tokens, 128)
        keep(pair, tokens, rows, attend(others, 0, pair))

    pl.loop(0, 2)(first_half)
    rings(7, 7)
    pl.loop(2, PAIRS)(first_half)
    rings(8, half)

    def back(pair, slot):
        return remote(
            obuf.at[pair, slot], rbuf.at[pair, slot], o_send.at[pair, slot], o_recv.at[pair, slot],
            in_plane(plane - slot),
        )

    def stat_back(slot):
        return remote(
            ostat_packed.at[slot], rstat_packed.at[slot], t_send.at[slot], t_recv.at[slot],
            in_plane(plane - slot),
        )

    ostat[...] = jnp.zeros_like(ostat)
    within = lax.rem(lane, HEAD_DIM)

    @pl.loop(0, PAIRS)
    def _(pair):
        out, largest, total = attend(qbuf[pair].reshape(rows, 128), half + 1, pair)
        old_largest = part_m[pair]
        top = jnp.maximum(largest, old_largest)
        now, before = jnp.exp(largest - top), jnp.exp(old_largest - top)
        out = (out * now + part_o[pair] * before).astype(BF16)
        total = total * now + part_l[pair] * before
        obuf[pair] = out.reshape(plane, tokens, 128)

        @pl.loop(1, plane)
        def _(slot):
            back(pair, slot).start()

        stats = jnp.where(within == pair, top, ostat[...])
        ostat[...] = jnp.where(within == pair + 8, total, stats)

    packs = tokens // 8
    tiles = ostat[...].reshape(plane, packs, 8, 128)
    packed = sum(
        pltpu.roll(tiles[:, pack].reshape(plane * 8, 128), 16 * pack, 1) if pack else tiles[:, pack].reshape(plane * 8, 128)
        for pack in range(packs)
    )
    ostat_packed[...] = packed.reshape(plane, 8, 128)

    @pl.loop(1, plane)
    def _(slot):
        stat_back(slot).start()

    head_lane = lax.broadcasted_iota(jnp.int32, (128, WIDTH), 0)
    feature = lax.broadcasted_iota(jnp.int32, (128, WIDTH), 1)
    from_feature = lax.rem(head_lane, HEAD_DIM) * 128 + (head_lane // HEAD_DIM) * HEAD_DIM
    spread = jnp.where((feature >= from_feature) & (feature < from_feature + HEAD_DIM), 1.0, 0.0).astype(BF16)
    rstat_packed[0] = ostat_packed[0]

    @pl.loop(1, plane)
    def _(slot):
        stat_back(slot).wait_recv()

    packed = rstat_packed[...].reshape(plane * 8, 128)
    tiles = [pltpu.roll(packed, 128 - 16 * pack, 1) if pack else packed for pack in range(packs)]
    stats = jnp.concatenate([tile.reshape(plane, 8, 128) for tile in tiles], axis=1)
    largest = jnp.max(stats, axis=0, keepdims=True)
    used = within < PAIRS
    weights = jnp.where(used, jnp.exp(stats - largest), 0.0)
    sums = pltpu.roll(stats.reshape(rows, 128), 120, 1).reshape(plane, tokens, 128)
    totals = jnp.where(used, jnp.sum(weights * sums, axis=0, keepdims=True), 1.0)
    shares = (weights / totals).reshape(rows, 128)
    upper = shares.astype(BF16)
    lower = (shares - upper.astype(F32)).astype(BF16)
    flat = jnp.dot(upper, spread, preferred_element_type=F32) + jnp.dot(lower, spread, preferred_element_type=F32)

    for pair in range(PAIRS):

        @pl.loop(1, plane)
        def _(slot):
            back(pair, slot).wait_recv()

        cols = slice(pair * 128, (pair + 1) * 128)
        scale = flat[:, cols].reshape(plane, tokens, 128)
        part = obuf[pair, 0].astype(F32) * scale[0]
        part = part + jnp.sum(rbuf[pair, 1:plane].astype(F32) * scale[1:], axis=0)
        result[0, :, cols] = part.astype(BF16)

    @pl.loop(1, plane)
    def _(step):
        stat1(step).wait_send()
        stat_back(step).wait_send()

        @pl.loop(0, PAIRS)
        def _(pair):
            share(pair, step).wait_send()
            back(pair, step).wait_send()

    @pl.loop(1, depth)
    def _(step):
        stat2(step).wait_send()

    for buf, send, recv, way, length in chains:
        for step in range(length):
            hop(buf, send, recv, way, step).wait_send()


def hand_over(result, att, fresh_keys, fresh_values, sems):
    copies = [
        pltpu.make_async_copy(result.at[i], out, sems.at[i])
        for i, out in enumerate((att, fresh_keys, fresh_values))
    ]
    for copy in copies:
        copy.start()
    for copy in copies:
        copy.wait()


def on_device(plane, x, gain, bias, wq, wk, wv, k, v):
    depth = lax.axis_size("rows") // plane
    tokens = x.shape[0]
    rows = plane * tokens
    dma = pltpu.SemaphoreType.DMA
    anywhere = pl.BlockSpec(memory_space=pltpu.HBM)
    local = pl.BlockSpec(memory_space=pltpu.VMEM)
    out = jax.ShapeDtypeStruct((tokens, WIDTH), BF16)
    result = pl.pallas_call(
        functools.partial(kernel, depth, plane, tokens),
        out_shape=pltpu.VMEM((3, tokens, WIDTH), BF16),
        in_specs=[anywhere, local, local] + [anywhere] * 5,
        out_specs=local,
        scratch_shapes=[
            pltpu.VMEM((tokens, CHANNELS), BF16),
            pltpu.VMEM((depth + 1, tokens, WIDTH), BF16),
            pltpu.VMEM((depth + 1, tokens, WIDTH), BF16),
            pltpu.VMEM((CHANNELS, WIDTH), BF16),
            pltpu.VMEM((CHANNELS, WIDTH), BF16),
            pltpu.VMEM((CHANNELS, WIDTH), BF16),
            pltpu.VMEM((CHANNELS, 128), BF16),
            pltpu.VMEM((PAIRS, plane, tokens, 128), BF16),
            pltpu.VMEM((plane, 2, 128), F32),
            pltpu.VMEM((depth, 2, 128), F32),
            pltpu.VMEM((PAIRS, rows, 128), F32),
            pltpu.VMEM((PAIRS, rows, 128), F32),
            pltpu.VMEM((PAIRS, rows, 128), F32),
            pltpu.VMEM((PAIRS, plane, tokens, 128), BF16),
            pltpu.VMEM((PAIRS, plane, tokens, 128), BF16),
            pltpu.VMEM((rows, 128), F32),
            pltpu.VMEM((plane, 8, 128), F32),
            pltpu.VMEM((plane, 8, 128), F32),
            dma((6,)),
            dma((plane,)), dma((plane,)), dma((depth,)), dma((depth,)),
            dma((PAIRS, plane)), dma((PAIRS, plane)),
            dma((2, depth)), dma((depth + 1,)), dma((2, depth)), dma((depth + 1,)),
            dma((PAIRS, plane)), dma((PAIRS, plane)),
            dma((plane,)), dma((plane,)),
        ],
        compiler_params=pltpu.CompilerParams(
            collective_id=0, has_side_effects=True, vmem_limit_bytes=60 * 1024 * 1024
        ),
        name="attention_of_plane",
    )(x, gain, bias, wq, wk, wv, k, v)
    return pl.pallas_call(
        hand_over,
        out_shape=(out, out, out),
        in_specs=[local],
        out_specs=(anywhere,) * 3,
        scratch_shapes=[dma((3,))],
        name="hand_over",
    )(result)


def solution(mesh, plane=PLANE):
    split = P(("batch", "rows"), None)
    return jax.shard_map(
        functools.partial(on_device, plane),
        mesh=mesh,
        in_specs=(split, P(), P(), P(), P(), P(), split, split),
        out_specs=(split, split, split),
        check_vma=False,
    )
```

```python
import functools

import jax
import jax.numpy as jnp
from jax import lax
from jax.experimental import pallas as pl
from jax.experimental.pallas import tpu as pltpu
from jax.sharding import PartitionSpec as P

CHANNELS = 1280
GROUPS = 32
GROUP_WIDTH = CHANNELS // GROUPS
HEADS = 10
HEAD_DIM = 64
WIDTH = HEADS * HEAD_DIM
PAIRS = HEADS // 2
EPSILON = 1e-05
PLANE = 8

F32 = jnp.float32
BF16 = jnp.bfloat16
MESH = pl.DeviceIdType.MESH
NT = (((1,), (1,)), ((), ()))


def exact_dot(value, right, dims):
    first = value.astype(BF16).astype(F32)
    second = (value - first).astype(BF16).astype(F32)
    terms = jnp.concatenate([first, second, value - first - second], axis=0).astype(BF16)
    out = lax.dot_general(terms, right, dims, preferred_element_type=F32)
    return out[0:8] + out[8:16] + out[16:24]


def to_groups(value, member):
    return exact_dot(value, member, (((1,), (0,)), ((), ())))


def to_channels(value, member):
    return exact_dot(value, member, NT)


def kernel(
    depth, plane, tokens,
    x_in, gain, bias, wq_in, wk_in, wv_in, k_in, v_in,
    result,
    x_own, kbuf, vbuf, wq, wk, wv, member, qbuf, st1, st2,
    part_o, part_m, part_l, obuf, rbuf, ostat, ostat_packed, rstat_packed,
    in_sem, s1_send, s1_recv, s2_send, s2_recv, q_send, q_recv,
    k_send, k_recv, v_send, v_recv, o_send, o_recv, t_send, t_recv,
):
    row = lax.axis_index("rows")
    z, p = row // plane, lax.rem(row, plane)
    half = depth // 2

    def in_plane(step):
        return {"rows": z * plane + lax.rem(p + step, plane)}

    def in_depth(step):
        return {"rows": lax.rem(z + step, depth) * plane + p}

    def remote(src, dst, send, recv, device):
        return pltpu.make_async_remote_copy(
            src_ref=src, dst_ref=dst, send_sem=send, recv_sem=recv,
            device_id=device, device_id_type=MESH,
        )

    barrier = pltpu.get_barrier_semaphore()

    @pl.loop(1, depth)
    def _(step):
        pl.semaphore_signal(barrier, inc=1, device_id=in_depth(step), device_id_type=MESH)

    @pl.loop(1, plane)
    def _(step):
        pl.semaphore_signal(barrier, inc=1, device_id=in_plane(step), device_id_type=MESH)

    loads = [
        pltpu.make_async_copy(src, dst, in_sem.at[i])
        for i, (src, dst) in enumerate(
            [(x_in, x_own), (k_in, kbuf.at[0]), (v_in, vbuf.at[0]),
             (wq_in, wq), (wk_in, wk), (wv_in, wv)]
        )
    ]
    for load in loads:
        load.start()

    channel = lax.broadcasted_iota(jnp.int32, (CHANNELS, 128), 0)
    group = lax.broadcasted_iota(jnp.int32, (CHANNELS, 128), 1)
    first = group * GROUP_WIDTH
    inside = (channel >= first) & (channel < first + GROUP_WIDTH) & (group < GROUPS)
    member[...] = jnp.where(inside, 1.0, 0.0).astype(BF16)

    loads[0].wait()
    x = x_own[...]
    count = tokens * GROUP_WIDTH
    mean = jnp.sum(jnp.dot(x, member[...], preferred_element_type=F32), axis=0, keepdims=True) / count
    centered = x.astype(F32) - to_channels(jnp.broadcast_to(mean, (8, 128)), member[...])[0:1]
    squares = jnp.sum((centered * centered).reshape(tokens // 8, 8, CHANNELS), axis=0)
    var = jnp.sum(to_groups(squares, member[...]), axis=0, keepdims=True) / count
    st1[0, 0:1, :] = mean
    st1[0, 1:2, :] = var
    loads[1].wait()
    loads[2].wait()

    pl.semaphore_wait(barrier, plane + depth - 2)

    def stat1(step):
        return remote(st1.at[0], st1.at[step], s1_send, s1_recv, in_plane(step))

    def stat2(step):
        return remote(st2.at[0], st2.at[step], s2_send, s2_recv, in_depth(step))

    def share(pair, step):
        return remote(
            qbuf.at[pair, 0], qbuf.at[pair, step], q_send.at[pair], q_recv.at[pair], in_plane(step)
        )

    def all_of(buf, send, recv):
        rest = buf.at[pl.ds(1, buf.shape[0] - 1)]
        return remote(rest, rest, send, recv, in_plane(1))

    order = [0]
    for step in range(1, half):
        order += [step, depth - step]
    order += [half]
    middle = half
    place = {block: at if at < middle else at + 1 for at, block in enumerate(order)}

    def hop(buf, send, recv, way, distance):
        before = distance - 1 if distance % 2 else distance - 2
        ends = [at if way == 0 else (depth - at) % depth for at in (before, distance)]
        by = distance - before if way == 0 else depth - (distance - before)
        here, there = place[ends[0]], place[ends[1]]
        return remote(buf.at[here], buf.at[there], send.at[way, distance], recv.at[there], in_depth(by))

    chains = [
        (kbuf, k_send, k_recv, 0, half),
        (vbuf, v_send, v_recv, 1, half),
        (kbuf, k_send, k_recv, 1, half - 1),
        (vbuf, v_send, v_recv, 0, half - 1),
    ]

    here_already = {0}

    def arrive(first, last):
        for distance in sorted(min(block, depth - block) for block in order[first:last]):
            if distance not in here_already:
                here_already.add(distance)
                for *chain, length in chains:
                    if distance <= length:
                        hop(*chain, distance).wait_recv()

    def forward(stop):
        here_already.add(stop)
        for *chain, length in chains:
            if 0 < stop <= length:
                hop(*chain, stop).wait_recv()
            for distance in (stop + 2, stop + 1):
                if distance <= length:
                    hop(*chain, distance).start()

    def merged(stats):
        means, spread = stats[:, 0, :], stats[:, 1, :]
        mean = jnp.mean(means, axis=0, keepdims=True)
        apart = means - mean
        return mean, jnp.mean(spread + apart * apart, axis=0, keepdims=True)

    @pl.loop(1, plane)
    def _(step):
        stat1(step).start()

    forward(0)
    all_of(st1, s1_send, s1_recv).wait_recv()

    mean, var = merged(st1[...])
    st2[0, 0:1, :] = mean
    st2[0, 1:2, :] = var

    @pl.loop(1, depth)
    def _(step):
        stat2(step).start()

    forward(2)
    all_of(st2, s2_send, s2_recv).wait_recv()

    mean, var = merged(st2[...])
    line = lax.broadcasted_iota(jnp.int32, (8, 128), 0)
    wide = to_channels(jnp.where(line == 0, mean, lax.rsqrt(var + EPSILON)), member[...])
    mean_chan = wide[0:1]
    scale_chan = wide[1:2] * gain[...].reshape(1, CHANNELS)
    bias_chan = bias[...].reshape(1, CHANNELS)
    normed = ((x_own[...].astype(F32) - mean_chan) * scale_chan + bias_chan).astype(BF16)

    loads[3].wait()
    query = jnp.dot(normed, wq[...], preferred_element_type=F32).astype(BF16)
    query = query * jnp.asarray(HEAD_DIM**-0.5, BF16)
    for pair in range(PAIRS):
        qbuf[pair, 0] = query[:, pair * 128 : (pair + 1) * 128]

    @pl.loop(0, PAIRS)
    def _(pair):
        @pl.loop(1, plane)
        def _(step):
            share(pair, step).start()

    forward(4)
    loads[4].wait()
    fresh = jnp.dot(normed, wk[...], preferred_element_type=F32).astype(BF16)
    kbuf[middle] = fresh
    result[1] = fresh
    loads[5].wait()
    fresh = jnp.dot(normed, wv[...], preferred_element_type=F32).astype(BF16)
    vbuf[middle] = fresh
    result[2] = fresh

    lane = lax.broadcasted_iota(jnp.int32, (1, 128), 1)
    low = lane < HEAD_DIM
    masks = (jnp.where(low, 1.0, 0.0).astype(BF16), jnp.where(low, 0.0, 1.0).astype(BF16))

    def attend(query, start, blocks, pair):
        cols = pl.ds(pl.multiple_of(pair * 128, 128), 128)
        keys_len = blocks * tokens
        keys = kbuf[start : start + blocks, :, cols].reshape(keys_len, 128)
        values = vbuf[start : start + blocks, :, cols].reshape(keys_len, 128)
        ones = jnp.ones((keys_len, 128), BF16)
        count = query.shape[0]
        both = jnp.concatenate([query * masks[0], query * masks[1]], axis=0)
        scores = lax.dot_general(both, keys, NT, preferred_element_type=F32)
        largest = jnp.max(scores, axis=-1, keepdims=True)
        exps = jnp.exp(scores - largest).astype(BF16)
        sums = jnp.dot(exps, jnp.concatenate([values, ones], axis=1), preferred_element_type=F32)

        def pick(tall):
            return jnp.where(low, tall[0:count], tall[count:])

        return pick(sums[:, 0:128]), pick(jnp.broadcast_to(largest, (2 * count, 128))), pick(sums[:, 128:])

    def keep(pair, first, last, parts):
        for buf, value in zip((part_o, part_m, part_l), parts):
            buf[pair, first:last] = value

    def add_to(pair, parts):
        out, largest, total = parts
        old_largest = part_m[pair]
        top = jnp.maximum(largest, old_largest)
        now, before = jnp.exp(largest - top), jnp.exp(old_largest - top)
        return out * now + part_o[pair] * before, top, total * now + part_l[pair] * before

    rows = plane * tokens
    quarter = half // 2

    arrive(0, half)

    @pl.loop(0, PAIRS)
    def _(pair):
        keep(pair, 0, tokens, attend(qbuf[pair, 0], 1, half, pair))

    def first_half(pair):
        all_of(qbuf.at[pair], q_send.at[pair], q_recv.at[pair]).wait_recv()
        others = qbuf[pair, 1:plane].reshape(rows - tokens, 128)
        keep(pair, tokens, rows, attend(others, 0, half, pair))

    pl.loop(0, 2)(first_half)
    if half > 4:
        forward(6)
    pl.loop(2, PAIRS)(first_half)
    arrive(half, half + quarter)

    @pl.loop(0, PAIRS)
    def _(pair):
        parts = attend(qbuf[pair].reshape(rows, 128), half + 1, quarter, pair)
        keep(pair, 0, rows, add_to(pair, parts))

    arrive(half + quarter, depth)

    def back(pair, slot):
        return remote(
            obuf.at[pair, slot], rbuf.at[pair, slot], o_send.at[pair], o_recv.at[pair],
            in_plane(plane - slot),
        )

    def stat_back(slot):
        return remote(
            ostat_packed.at[slot], rstat_packed.at[slot], t_send, t_recv, in_plane(plane - slot)
        )

    ostat[...] = jnp.zeros_like(ostat)
    within = lax.rem(lane, HEAD_DIM)

    @pl.loop(0, PAIRS)
    def _(pair):
        parts = attend(qbuf[pair].reshape(rows, 128), half + 1 + quarter, quarter, pair)
        out, top, total = add_to(pair, parts)
        obuf[pair] = out.astype(BF16).reshape(plane, tokens, 128)

        @pl.loop(1, plane)
        def _(slot):
            back(pair, slot).start()

        stats = jnp.where(within == pair, top, ostat[...])
        ostat[...] = jnp.where(within == pair + 8, total, stats)

    packs = tokens // 8
    tiles = ostat[...].reshape(plane, packs, 8, 128)
    packed = sum(
        pltpu.roll(tiles[:, pack].reshape(plane * 8, 128), 16 * pack, 1) if pack else tiles[:, pack].reshape(plane * 8, 128)
        for pack in range(packs)
    )
    ostat_packed[...] = packed.reshape(plane, 8, 128)

    @pl.loop(1, plane)
    def _(slot):
        stat_back(slot).start()

    head_lane = lax.broadcasted_iota(jnp.int32, (128, WIDTH), 0)
    feature = lax.broadcasted_iota(jnp.int32, (128, WIDTH), 1)
    from_feature = lax.rem(head_lane, HEAD_DIM) * 128 + (head_lane // HEAD_DIM) * HEAD_DIM
    spread = jnp.where((feature >= from_feature) & (feature < from_feature + HEAD_DIM), 1.0, 0.0).astype(BF16)
    rstat_packed[0] = ostat_packed[0]

    all_of(st1, s1_send, s1_recv).wait_send()
    all_of(st2, s2_send, s2_recv).wait_send()
    for *chain, length in chains:
        for distance in range(1, length + 1):
            hop(*chain, distance).wait_send()
    for pair in range(PAIRS):
        all_of(qbuf.at[pair], q_send.at[pair], q_recv.at[pair]).wait_send()

    all_of(rstat_packed, t_send, t_recv).wait_recv()
    packed = rstat_packed[...].reshape(plane * 8, 128)
    tiles = [pltpu.roll(packed, 128 - 16 * pack, 1) if pack else packed for pack in range(packs)]
    stats = jnp.concatenate([tile.reshape(plane, 8, 128) for tile in tiles], axis=1)
    largest = jnp.max(stats, axis=0, keepdims=True)
    used = within < PAIRS
    weights = jnp.where(used, jnp.exp(stats - largest), 0.0)
    sums = pltpu.roll(stats.reshape(rows, 128), 120, 1).reshape(plane, tokens, 128)
    totals = jnp.where(used, jnp.sum(weights * sums, axis=0, keepdims=True), 1.0)
    shares = (weights / totals).reshape(rows, 128)
    upper = shares.astype(BF16)
    lower = (shares - upper.astype(F32)).astype(BF16)
    flat = jnp.dot(upper, spread, preferred_element_type=F32) + jnp.dot(lower, spread, preferred_element_type=F32)

    for pair in range(PAIRS):
        all_of(rbuf.at[pair], o_send.at[pair], o_recv.at[pair]).wait_recv()
        cols = slice(pair * 128, (pair + 1) * 128)
        scale = flat[:, cols].reshape(plane, tokens, 128)
        part = obuf[pair, 0].astype(F32) * scale[0]
        part = part + jnp.sum(rbuf[pair, 1:plane].astype(F32) * scale[1:], axis=0)
        result[0, :, cols] = part.astype(BF16)

    for pair in range(PAIRS):
        all_of(obuf.at[pair], o_send.at[pair], o_recv.at[pair]).wait_send()
    all_of(ostat_packed, t_send, t_recv).wait_send()


def hand_over(result, att, fresh_keys, fresh_values, sems):
    copies = [
        pltpu.make_async_copy(result.at[i], out, sems.at[i])
        for i, out in enumerate((att, fresh_keys, fresh_values))
    ]
    for copy in copies:
        copy.start()
    for copy in copies:
        copy.wait()


def on_device(plane, x, gain, bias, wq, wk, wv, k, v):
    depth = lax.axis_size("rows") // plane
    tokens = x.shape[0]
    rows = plane * tokens
    dma = pltpu.SemaphoreType.DMA
    anywhere = pl.BlockSpec(memory_space=pltpu.HBM)
    local = pl.BlockSpec(memory_space=pltpu.VMEM)
    out = jax.ShapeDtypeStruct((tokens, WIDTH), BF16)
    result = pl.pallas_call(
        functools.partial(kernel, depth, plane, tokens),
        out_shape=pltpu.VMEM((3, tokens, WIDTH), BF16),
        in_specs=[anywhere, local, local] + [anywhere] * 5,
        out_specs=local,
        scratch_shapes=[
            pltpu.VMEM((tokens, CHANNELS), BF16),
            pltpu.VMEM((depth + 1, tokens, WIDTH), BF16),
            pltpu.VMEM((depth + 1, tokens, WIDTH), BF16),
            pltpu.VMEM((CHANNELS, WIDTH), BF16),
            pltpu.VMEM((CHANNELS, WIDTH), BF16),
            pltpu.VMEM((CHANNELS, WIDTH), BF16),
            pltpu.VMEM((CHANNELS, 128), BF16),
            pltpu.VMEM((PAIRS, plane, tokens, 128), BF16),
            pltpu.VMEM((plane, 2, 128), F32),
            pltpu.VMEM((depth, 2, 128), F32),
            pltpu.VMEM((PAIRS, rows, 128), F32),
            pltpu.VMEM((PAIRS, rows, 128), F32),
            pltpu.VMEM((PAIRS, rows, 128), F32),
            pltpu.VMEM((PAIRS, plane, tokens, 128), BF16),
            pltpu.VMEM((PAIRS, plane, tokens, 128), BF16),
            pltpu.VMEM((rows, 128), F32),
            pltpu.VMEM((plane, 8, 128), F32),
            pltpu.VMEM((plane, 8, 128), F32),
            dma((6,)),
            dma, dma, dma, dma,
            dma((PAIRS,)), dma((PAIRS,)),
            dma((2, depth)), dma((depth + 1,)), dma((2, depth)), dma((depth + 1,)),
            dma((PAIRS,)), dma((PAIRS,)),
            dma, dma,
        ],
        compiler_params=pltpu.CompilerParams(
            collective_id=0, has_side_effects=True, vmem_limit_bytes=60 * 1024 * 1024
        ),
        name="attention_of_plane",
    )(x, gain, bias, wq, wk, wv, k, v)
    return pl.pallas_call(
        hand_over,
        out_shape=(out, out, out),
        in_specs=[local],
        out_specs=(anywhere,) * 3,
        scratch_shapes=[dma((3,))],
        name="hand_over",
    )(pltpu.with_memory_space_constraint(result, pltpu.VMEM))


def solution(mesh, plane=PLANE):
    split = P(("batch", "rows"), None)
    return jax.shard_map(
        functools.partial(on_device, plane),
        mesh=mesh,
        in_specs=(split, P(), P(), P(), P(), P(), split, split),
        out_specs=(split, split, split),
        check_vma=False,
    )
```

```python
import functools

import jax
import jax.numpy as jnp
from jax import lax
from jax.experimental import pallas as pl
from jax.experimental.pallas import tpu as pltpu
from jax.sharding import PartitionSpec as P

CHANNELS = 1280
GROUPS = 32
GROUP_WIDTH = CHANNELS // GROUPS
HEADS = 10
HEAD_DIM = 64
WIDTH = HEADS * HEAD_DIM
PAIRS = HEADS // 2
EPSILON = 1e-05
PLANE = 8

F32 = jnp.float32
BF16 = jnp.bfloat16
MESH = pl.DeviceIdType.MESH
NT = (((1,), (1,)), ((), ()))


def exact_dot(value, right, dims):
    first = value.astype(BF16).astype(F32)
    second = (value - first).astype(BF16).astype(F32)
    terms = jnp.concatenate([first, second, value - first - second], axis=0).astype(BF16)
    out = lax.dot_general(terms, right, dims, preferred_element_type=F32)
    return out[0:8] + out[8:16] + out[16:24]


def to_groups(value, member):
    return exact_dot(value, member, (((1,), (0,)), ((), ())))


def to_channels(value, member):
    return exact_dot(value, member, NT)


def kernel(
    depth, plane, tokens,
    x_in, gain, bias, wq_in, wk_in, wv_in, k_in, v_in,
    result,
    x_own, kbuf, vbuf, wq, wk, wv, member, qbuf, st1, st2,
    part_o, part_m, part_l, obuf, rbuf, ostat, ostat_packed, rstat_packed,
    in_sem, s1_send, s1_recv, s2_send, s2_recv, q_send, q_recv,
    k_send, k_recv, v_send, v_recv, o_send, o_recv, t_send, t_recv,
):
    row = lax.axis_index("rows")
    z, p = row // plane, lax.rem(row, plane)
    half = depth // 2

    def in_plane(step):
        return {"rows": z * plane + lax.rem(p + step, plane)}

    def in_depth(step):
        return {"rows": lax.rem(z + step, depth) * plane + p}

    def remote(src, dst, send, recv, device):
        return pltpu.make_async_remote_copy(
            src_ref=src, dst_ref=dst, send_sem=send, recv_sem=recv,
            device_id=device, device_id_type=MESH,
        )

    barrier = pltpu.get_barrier_semaphore()

    @pl.loop(1, depth)
    def _(step):
        pl.semaphore_signal(barrier, inc=1, device_id=in_depth(step), device_id_type=MESH)

    @pl.loop(1, plane)
    def _(step):
        pl.semaphore_signal(barrier, inc=1, device_id=in_plane(step), device_id_type=MESH)

    loads = [
        pltpu.make_async_copy(src, dst, in_sem.at[i])
        for i, (src, dst) in enumerate(
            [(k_in, kbuf.at[0]), (v_in, vbuf.at[0]), (x_in, x_own),
             (wq_in, wq), (wk_in, wk), (wv_in, wv)]
        )
    ]
    for load in loads:
        load.start()

    channel = lax.broadcasted_iota(jnp.int32, (CHANNELS, 128), 0)
    group = lax.broadcasted_iota(jnp.int32, (CHANNELS, 128), 1)
    first = group * GROUP_WIDTH
    inside = (channel >= first) & (channel < first + GROUP_WIDTH) & (group < GROUPS)
    member[...] = jnp.where(inside, 1.0, 0.0).astype(BF16)

    loads[0].wait()
    loads[1].wait()
    pl.semaphore_wait(barrier, plane + depth - 2)

    def stat1(step):
        return remote(st1.at[0], st1.at[step], s1_send, s1_recv, in_plane(step))

    def stat2(step):
        return remote(st2.at[0], st2.at[step], s2_send, s2_recv, in_depth(step))

    def share(pair, step):
        return remote(
            qbuf.at[pair, 0], qbuf.at[pair, step], q_send.at[pair], q_recv.at[pair], in_plane(step)
        )

    def all_of(buf, send, recv):
        rest = buf.at[pl.ds(1, buf.shape[0] - 1)]
        return remote(rest, rest, send, recv, in_plane(1))

    order = [0]
    for step in range(1, half):
        order += [step, depth - step]
    order += [half]
    middle = half
    place = {block: at if at < middle else at + 1 for at, block in enumerate(order)}

    def hop(buf, send, recv, way, distance):
        before = distance - 1 if distance % 2 else distance - 2
        ends = [at if way == 0 else (depth - at) % depth for at in (before, distance)]
        by = distance - before if way == 0 else depth - (distance - before)
        here, there = place[ends[0]], place[ends[1]]
        return remote(buf.at[here], buf.at[there], send.at[way, distance], recv.at[there], in_depth(by))

    chains = [
        (kbuf, k_send, k_recv, 0, half),
        (vbuf, v_send, v_recv, 1, half),
        (kbuf, k_send, k_recv, 1, half - 1),
        (vbuf, v_send, v_recv, 0, half - 1),
    ]

    here_already = {0}

    def arrive(first, last):
        for distance in sorted(min(block, depth - block) for block in order[first:last]):
            if distance not in here_already:
                here_already.add(distance)
                for *chain, length in chains:
                    if distance <= length:
                        hop(*chain, distance).wait_recv()

    def forward(stop):
        here_already.add(stop)
        for *chain, length in chains:
            if 0 < stop <= length:
                hop(*chain, stop).wait_recv()
            for distance in (stop + 2, stop + 1):
                if distance <= length:
                    hop(*chain, distance).start()

    def merged(stats):
        means, spread = stats[:, 0, :], stats[:, 1, :]
        mean = jnp.mean(means, axis=0, keepdims=True)
        apart = means - mean
        return mean, jnp.mean(spread + apart * apart, axis=0, keepdims=True)

    forward(0)

    loads[2].wait()
    x = x_own[...]
    count = tokens * GROUP_WIDTH
    mean = jnp.sum(jnp.dot(x, member[...], preferred_element_type=F32), axis=0, keepdims=True) / count
    centered = x.astype(F32) - to_channels(jnp.broadcast_to(mean, (8, 128)), member[...])[0:1]
    squares = jnp.sum((centered * centered).reshape(tokens // 8, 8, CHANNELS), axis=0)
    var = jnp.sum(to_groups(squares, member[...]), axis=0, keepdims=True) / count
    st1[0, 0:1, :] = mean
    st1[0, 1:2, :] = var

    @pl.loop(1, plane)
    def _(step):
        stat1(step).start()

    all_of(st1, s1_send, s1_recv).wait_recv()

    mean, var = merged(st1[...])
    st2[0, 0:1, :] = mean
    st2[0, 1:2, :] = var

    @pl.loop(1, depth)
    def _(step):
        stat2(step).start()

    forward(2)
    all_of(st2, s2_send, s2_recv).wait_recv()

    mean, var = merged(st2[...])
    line = lax.broadcasted_iota(jnp.int32, (8, 128), 0)
    wide = to_channels(jnp.where(line == 0, mean, lax.rsqrt(var + EPSILON)), member[...])
    mean_chan = wide[0:1]
    scale_chan = wide[1:2] * gain[...].reshape(1, CHANNELS)
    bias_chan = bias[...].reshape(1, CHANNELS)
    normed = ((x_own[...].astype(F32) - mean_chan) * scale_chan + bias_chan).astype(BF16)

    loads[3].wait()
    query = jnp.dot(normed, wq[...], preferred_element_type=F32).astype(BF16)
    query = query * jnp.asarray(HEAD_DIM**-0.5, BF16)
    for pair in range(PAIRS):
        qbuf[pair, 0] = query[:, pair * 128 : (pair + 1) * 128]

    @pl.loop(0, PAIRS)
    def _(pair):
        @pl.loop(1, plane)
        def _(step):
            share(pair, step).start()

    forward(4)
    loads[4].wait()
    fresh = jnp.dot(normed, wk[...], preferred_element_type=F32).astype(BF16)
    kbuf[middle] = fresh
    result[1] = fresh
    loads[5].wait()
    fresh = jnp.dot(normed, wv[...], preferred_element_type=F32).astype(BF16)
    vbuf[middle] = fresh
    result[2] = fresh

    lane = lax.broadcasted_iota(jnp.int32, (1, 128), 1)
    low = lane < HEAD_DIM
    masks = (jnp.where(low, 1.0, 0.0).astype(BF16), jnp.where(low, 0.0, 1.0).astype(BF16))

    def columns(buf, start, blocks, pair):
        return buf[start : start + blocks, :, pair * 128 : (pair + 1) * 128].reshape(blocks * tokens, 128)

    def scored(query, start, blocks, pair):
        both = jnp.concatenate([query * masks[0], query * masks[1]], axis=0)
        keys = columns(kbuf, start, blocks, pair)
        scores = lax.dot_general(both, keys, NT, preferred_element_type=F32)
        largest = jnp.max(scores, axis=-1, keepdims=True)
        return jnp.exp(scores - largest).astype(BF16), largest

    def valued(exps, largest, start, blocks, pair):
        ones = jnp.ones((blocks * tokens, 128), BF16)
        right = jnp.concatenate([columns(vbuf, start, blocks, pair), ones], axis=1)
        sums = jnp.dot(exps, right, preferred_element_type=F32)
        count = exps.shape[0] // 2

        def pick(tall):
            return jnp.where(low, tall[0:count], tall[count:])

        return pick(sums[:, 0:128]), pick(jnp.broadcast_to(largest, (2 * count, 128))), pick(sums[:, 128:])

    def attend(query_of, start, blocks, pairs, take):
        waiting = None
        for pair in list(pairs) + [None]:
            ready = waiting
            waiting = None if pair is None else (*scored(query_of(pair), start, blocks, pair), start, blocks, pair)
            if ready is not None:
                take(ready[-1], valued(*ready))

    def keep(pair, first, last, parts):
        for buf, value in zip((part_o, part_m, part_l), parts):
            buf[pair, first:last] = value

    def add_to(pair, parts):
        out, largest, total = parts
        old_largest = part_m[pair]
        top = jnp.maximum(largest, old_largest)
        now, before = jnp.exp(largest - top), jnp.exp(old_largest - top)
        return out * now + part_o[pair] * before, top, total * now + part_l[pair] * before

    rows = plane * tokens
    quarter = half // 2

    arrive(0, half)

    attend(
        lambda pair: qbuf[pair, 0], 1, half, range(PAIRS),
        lambda pair, parts: keep(pair, 0, tokens, parts),
    )

    def first_half(pairs):
        for pair in pairs:
            all_of(qbuf.at[pair], q_send.at[pair], q_recv.at[pair]).wait_recv()
        attend(
            lambda pair: qbuf[pair, 1:plane].reshape(rows - tokens, 128), 0, half, pairs,
            lambda pair, parts: keep(pair, tokens, rows, parts),
        )

    first_half(range(0, 2))
    if half > 4:
        forward(6)
    first_half(range(2, PAIRS))
    arrive(half, half + quarter)

    def all_queries(pair):
        return qbuf[pair].reshape(rows, 128)

    attend(
        all_queries, half + 1, quarter, range(PAIRS),
        lambda pair, parts: keep(pair, 0, rows, add_to(pair, parts)),
    )
    arrive(half + quarter, depth)

    def back(pair, slot):
        return remote(
            obuf.at[pair, slot], rbuf.at[pair, slot], o_send.at[pair], o_recv.at[pair],
            in_plane(plane - slot),
        )

    def stat_back(slot):
        return remote(
            ostat_packed.at[slot], rstat_packed.at[slot], t_send, t_recv, in_plane(plane - slot)
        )

    ostat[...] = jnp.zeros_like(ostat)
    within = lax.rem(lane, HEAD_DIM)

    def send_back(pair, parts):
        out, top, total = add_to(pair, parts)
        obuf[pair] = out.astype(BF16).reshape(plane, tokens, 128)
        for slot in range(1, plane):
            back(pair, slot).start()
        stats = jnp.where(within == pair, top, ostat[...])
        ostat[...] = jnp.where(within == pair + 8, total, stats)

    attend(all_queries, half + 1 + quarter, quarter, range(PAIRS), send_back)

    packs = tokens // 8
    tiles = ostat[...].reshape(plane, packs, 8, 128)
    packed = sum(
        pltpu.roll(tiles[:, pack].reshape(plane * 8, 128), 16 * pack, 1) if pack else tiles[:, pack].reshape(plane * 8, 128)
        for pack in range(packs)
    )
    ostat_packed[...] = packed.reshape(plane, 8, 128)

    @pl.loop(1, plane)
    def _(slot):
        stat_back(slot).start()

    head_lane = lax.broadcasted_iota(jnp.int32, (128, WIDTH), 0)
    feature = lax.broadcasted_iota(jnp.int32, (128, WIDTH), 1)
    from_feature = lax.rem(head_lane, HEAD_DIM) * 128 + (head_lane // HEAD_DIM) * HEAD_DIM
    spread = jnp.where((feature >= from_feature) & (feature < from_feature + HEAD_DIM), 1.0, 0.0).astype(BF16)
    rstat_packed[0] = ostat_packed[0]

    all_of(st1, s1_send, s1_recv).wait_send()
    all_of(st2, s2_send, s2_recv).wait_send()
    for *chain, length in chains:
        for distance in range(1, length + 1):
            hop(*chain, distance).wait_send()
    for pair in range(PAIRS):
        all_of(qbuf.at[pair], q_send.at[pair], q_recv.at[pair]).wait_send()

    all_of(rstat_packed, t_send, t_recv).wait_recv()
    packed = rstat_packed[...].reshape(plane * 8, 128)
    tiles = [pltpu.roll(packed, 128 - 16 * pack, 1) if pack else packed for pack in range(packs)]
    stats = jnp.concatenate([tile.reshape(plane, 8, 128) for tile in tiles], axis=1)
    largest = jnp.max(stats, axis=0, keepdims=True)
    used = within < PAIRS
    weights = jnp.where(used, jnp.exp(stats - largest), 0.0)
    sums = pltpu.roll(stats.reshape(rows, 128), 120, 1).reshape(plane, tokens, 128)
    totals = jnp.where(used, jnp.sum(weights * sums, axis=0, keepdims=True), 1.0)
    shares = (weights / totals).reshape(rows, 128)
    upper = shares.astype(BF16)
    lower = (shares - upper.astype(F32)).astype(BF16)
    flat = jnp.dot(upper, spread, preferred_element_type=F32) + jnp.dot(lower, spread, preferred_element_type=F32)

    for pair in range(PAIRS):
        all_of(rbuf.at[pair], o_send.at[pair], o_recv.at[pair]).wait_recv()
        cols = slice(pair * 128, (pair + 1) * 128)
        scale = flat[:, cols].reshape(plane, tokens, 128)
        part = obuf[pair, 0].astype(F32) * scale[0]
        part = part + jnp.sum(rbuf[pair, 1:plane].astype(F32) * scale[1:], axis=0)
        result[0, :, cols] = part.astype(BF16)

    for pair in range(PAIRS):
        all_of(obuf.at[pair], o_send.at[pair], o_recv.at[pair]).wait_send()
    all_of(ostat_packed, t_send, t_recv).wait_send()


def hand_over(result, att, fresh_keys, fresh_values, sems):
    copies = [
        pltpu.make_async_copy(result.at[i], out, sems.at[i])
        for i, out in enumerate((att, fresh_keys, fresh_values))
    ]
    for copy in copies:
        copy.start()
    for copy in copies:
        copy.wait()


def on_device(plane, x, gain, bias, wq, wk, wv, k, v):
    depth = lax.axis_size("rows") // plane
    tokens = x.shape[0]
    rows = plane * tokens
    dma = pltpu.SemaphoreType.DMA
    anywhere = pl.BlockSpec(memory_space=pltpu.HBM)
    local = pl.BlockSpec(memory_space=pltpu.VMEM)
    out = jax.ShapeDtypeStruct((tokens, WIDTH), BF16)
    result = pl.pallas_call(
        functools.partial(kernel, depth, plane, tokens),
        out_shape=pltpu.VMEM((3, tokens, WIDTH), BF16),
        in_specs=[anywhere, local, local] + [anywhere] * 5,
        out_specs=local,
        scratch_shapes=[
            pltpu.VMEM((tokens, CHANNELS), BF16),
            pltpu.VMEM((depth + 1, tokens, WIDTH), BF16),
            pltpu.VMEM((depth + 1, tokens, WIDTH), BF16),
            pltpu.VMEM((CHANNELS, WIDTH), BF16),
            pltpu.VMEM((CHANNELS, WIDTH), BF16),
            pltpu.VMEM((CHANNELS, WIDTH), BF16),
            pltpu.VMEM((CHANNELS, 128), BF16),
            pltpu.VMEM((PAIRS, plane, tokens, 128), BF16),
            pltpu.VMEM((plane, 2, 128), F32),
            pltpu.VMEM((depth, 2, 128), F32),
            pltpu.VMEM((PAIRS, rows, 128), F32),
            pltpu.VMEM((PAIRS, rows, 128), F32),
            pltpu.VMEM((PAIRS, rows, 128), F32),
            pltpu.VMEM((PAIRS, plane, tokens, 128), BF16),
            pltpu.VMEM((PAIRS, plane, tokens, 128), BF16),
            pltpu.VMEM((rows, 128), F32),
            pltpu.VMEM((plane, 8, 128), F32),
            pltpu.VMEM((plane, 8, 128), F32),
            dma((6,)),
            dma, dma, dma, dma,
            dma((PAIRS,)), dma((PAIRS,)),
            dma((2, depth)), dma((depth + 1,)), dma((2, depth)), dma((depth + 1,)),
            dma((PAIRS,)), dma((PAIRS,)),
            dma, dma,
        ],
        compiler_params=pltpu.CompilerParams(
            collective_id=0, has_side_effects=True, vmem_limit_bytes=60 * 1024 * 1024
        ),
        name="attention_of_plane",
    )(x, gain, bias, wq, wk, wv, k, v)
    return pl.pallas_call(
        hand_over,
        out_shape=(out, out, out),
        in_specs=[local],
        out_specs=(anywhere,) * 3,
        scratch_shapes=[dma((3,))],
        name="hand_over",
    )(pltpu.with_memory_space_constraint(result, pltpu.VMEM))


def solution(mesh, plane=PLANE):
    split = P(("batch", "rows"), None)
    return jax.shard_map(
        functools.partial(on_device, plane),
        mesh=mesh,
        in_specs=(split, P(), P(), P(), P(), P(), split, split),
        out_specs=(split, split, split),
        check_vma=False,
    )
```

```python
import functools

import jax
import jax.numpy as jnp
from jax import lax
from jax.experimental import pallas as pl
from jax.experimental.pallas import tpu as pltpu
from jax.sharding import PartitionSpec as P

CHANNELS = 1280
GROUPS = 32
GROUP_WIDTH = CHANNELS // GROUPS
HEADS = 10
HEAD_DIM = 64
WIDTH = HEADS * HEAD_DIM
PAIRS = HEADS // 2
EPSILON = 1e-05
PLANE = 8

F32 = jnp.float32
BF16 = jnp.bfloat16
MESH = pl.DeviceIdType.MESH
NT = (((1,), (1,)), ((), ()))


def exact_dot(value, right, dims):
    first = value.astype(BF16).astype(F32)
    second = (value - first).astype(BF16).astype(F32)
    terms = jnp.concatenate([first, second, value - first - second], axis=0).astype(BF16)
    out = lax.dot_general(terms, right, dims, preferred_element_type=F32)
    return out[0:8] + out[8:16] + out[16:24]


def to_groups(value, member):
    return exact_dot(value, member, (((1,), (0,)), ((), ())))


def to_channels(value, member):
    return exact_dot(value, member, NT)


def kernel(
    depth, plane, tokens,
    x_in, gain, bias, wq_in, wk_in, wv_in, k_in, v_in,
    result,
    x_own, kv, wq, wk, wv, member, qbuf, st1, st2,
    part_o, part_m, part_l, obuf, rbuf, ostat, ostat_packed, rstat_packed,
    in_sem, kv_sem, s1_send, s1_recv, s2_send, s2_recv, q_send, q_recv,
    kv_send, kv_recv, o_send, o_recv, t_send, t_recv,
):
    row = lax.axis_index("rows")
    z, p = row // plane, lax.rem(row, plane)
    half = depth // 2

    def in_plane(step):
        return {"rows": z * plane + lax.rem(p + step, plane)}

    def in_depth(step):
        return {"rows": lax.rem(z + step, depth) * plane + p}

    def remote(src, dst, send, recv, device):
        return pltpu.make_async_remote_copy(
            src_ref=src, dst_ref=dst, send_sem=send, recv_sem=recv,
            device_id=device, device_id_type=MESH,
        )

    barrier = pltpu.get_barrier_semaphore()

    @pl.loop(1, depth)
    def _(step):
        pl.semaphore_signal(barrier, inc=1, device_id=in_depth(step), device_id_type=MESH)

    @pl.loop(1, plane)
    def _(step):
        pl.semaphore_signal(barrier, inc=1, device_id=in_plane(step), device_id_type=MESH)

    blocks_in = [
        pltpu.make_async_copy(src.at[:, pl.ds(pair * 128, 128)], kv.at[0, pair, kind], kv_sem.at[pair, kind])
        for pair in range(PAIRS)
        for kind, src in enumerate((k_in, v_in))
    ]
    loads = [
        pltpu.make_async_copy(src, dst, in_sem.at[i])
        for i, (src, dst) in enumerate([(x_in, x_own), (wq_in, wq), (wk_in, wk), (wv_in, wv)])
    ]
    for load in blocks_in + loads:
        load.start()

    channel = lax.broadcasted_iota(jnp.int32, (CHANNELS, 128), 0)
    group = lax.broadcasted_iota(jnp.int32, (CHANNELS, 128), 1)
    first = group * GROUP_WIDTH
    inside = (channel >= first) & (channel < first + GROUP_WIDTH) & (group < GROUPS)
    member[...] = jnp.where(inside, 1.0, 0.0).astype(BF16)

    for load in blocks_in:
        load.wait()
    pl.semaphore_wait(barrier, plane + depth - 2)

    def stat1(step):
        return remote(st1.at[0], st1.at[step], s1_send, s1_recv, in_plane(step))

    def stat2(step):
        return remote(st2.at[0], st2.at[step], s2_send, s2_recv, in_depth(step))

    def share(pair, step):
        return remote(
            qbuf.at[pair, 0], qbuf.at[pair, step], q_send.at[pair], q_recv.at[pair], in_plane(step)
        )

    def all_of(buf, send, recv):
        rest = buf.at[pl.ds(1, buf.shape[0] - 1)]
        return remote(rest, rest, send, recv, in_plane(1))

    order = [0]
    for step in range(1, half):
        order += [step, depth - step]
    order += [half]
    middle = half
    place = {block: at if at < middle else at + 1 for at, block in enumerate(order)}

    def hop(way, pair, distance):
        before = distance - 1 if distance % 2 else distance - 2
        ends = [at if way == 0 else (depth - at) % depth for at in (before, distance)]
        by = distance - before if way == 0 else depth - (distance - before)
        here, there = place[ends[0]], place[ends[1]]
        return remote(kv.at[here, pair], kv.at[there, pair], kv_send, kv_recv.at[there, pair], in_depth(by))

    def length(way, pair):
        return half if pair % 2 == way else half - 1

    both_ways = (0, 1)
    pairs_all = range(PAIRS)
    seen = {(0, pair) for pair in pairs_all}

    def arrive(distance, pair):
        if (distance, pair) not in seen:
            seen.add((distance, pair))
            for way in both_ways:
                if distance <= length(way, pair):
                    hop(way, pair, distance).wait_recv()

    def need(first, last, pairs):
        for pair in pairs:
            for distance in sorted(min(block, depth - block) for block in order[first:last]):
                arrive(distance, pair)

    def forward(stop, pairs):
        if stop >= half:
            return
        for by in (2, 1):
            for pair in pairs:
                arrive(stop, pair)
                for way in both_ways:
                    if stop + by <= length(way, pair):
                        hop(way, pair, stop + by).start()

    def merged(stats):
        means, spread = stats[:, 0, :], stats[:, 1, :]
        mean = jnp.mean(means, axis=0, keepdims=True)
        apart = means - mean
        return mean, jnp.mean(spread + apart * apart, axis=0, keepdims=True)

    forward(0, pairs_all)

    loads[0].wait()
    x = x_own[...]
    count = tokens * GROUP_WIDTH
    mean = jnp.sum(jnp.dot(x, member[...], preferred_element_type=F32), axis=0, keepdims=True) / count
    centered = x.astype(F32) - to_channels(jnp.broadcast_to(mean, (8, 128)), member[...])[0:1]
    squares = jnp.sum((centered * centered).reshape(tokens // 8, 8, CHANNELS), axis=0)
    var = jnp.sum(to_groups(squares, member[...]), axis=0, keepdims=True) / count
    st1[0, 0:1, :] = mean
    st1[0, 1:2, :] = var

    @pl.loop(1, plane)
    def _(step):
        stat1(step).start()

    forward(2, range(0, 2))
    all_of(st1, s1_send, s1_recv).wait_recv()

    mean, var = merged(st1[...])
    st2[0, 0:1, :] = mean
    st2[0, 1:2, :] = var

    @pl.loop(1, depth)
    def _(step):
        stat2(step).start()

    forward(2, range(2, PAIRS))
    forward(4, range(0, 3))
    all_of(st2, s2_send, s2_recv).wait_recv()

    mean, var = merged(st2[...])
    forward(4, range(3, PAIRS))
    line = lax.broadcasted_iota(jnp.int32, (8, 128), 0)
    wide = to_channels(jnp.where(line == 0, mean, lax.rsqrt(var + EPSILON)), member[...])
    mean_chan = wide[0:1]
    scale_chan = wide[1:2] * gain[...].reshape(1, CHANNELS)
    bias_chan = bias[...].reshape(1, CHANNELS)
    normed = ((x_own[...].astype(F32) - mean_chan) * scale_chan + bias_chan).astype(BF16)

    loads[1].wait()
    query = jnp.dot(normed, wq[...], preferred_element_type=F32).astype(BF16)
    query = query * jnp.asarray(HEAD_DIM**-0.5, BF16)
    for pair in range(PAIRS):
        qbuf[pair, 0] = query[:, pair * 128 : (pair + 1) * 128]

    @pl.loop(0, PAIRS)
    def _(pair):
        @pl.loop(1, plane)
        def _(step):
            share(pair, step).start()

    forward(6, range(0, 3))
    loads[2].wait()
    fresh = jnp.dot(normed, wk[...], preferred_element_type=F32).astype(BF16)
    for pair in range(PAIRS):
        kv[middle, pair, 0] = fresh[:, pair * 128 : (pair + 1) * 128]
    result[1] = fresh
    loads[3].wait()
    fresh = jnp.dot(normed, wv[...], preferred_element_type=F32).astype(BF16)
    for pair in range(PAIRS):
        kv[middle, pair, 1] = fresh[:, pair * 128 : (pair + 1) * 128]
    result[2] = fresh
    forward(6, range(3, PAIRS))
    need(0, half, pairs_all)

    lane = lax.broadcasted_iota(jnp.int32, (1, 128), 1)
    low = lane < HEAD_DIM
    masks = (jnp.where(low, 1.0, 0.0).astype(BF16), jnp.where(low, 0.0, 1.0).astype(BF16))

    def gathered(kind, start, blocks, pair):
        return kv[start : start + blocks, pair, kind].reshape(blocks * tokens, 128)

    def scored(query, start, blocks, pair):
        both = jnp.concatenate([query * masks[0], query * masks[1]], axis=0)
        keys = gathered(0, start, blocks, pair)
        scores = lax.dot_general(both, keys, NT, preferred_element_type=F32)
        largest = jnp.max(scores, axis=-1, keepdims=True)
        return jnp.exp(scores - largest).astype(BF16), largest

    def valued(exps, largest, start, blocks, pair):
        ones = jnp.ones((blocks * tokens, 128), BF16)
        right = jnp.concatenate([gathered(1, start, blocks, pair), ones], axis=1)
        sums = jnp.dot(exps, right, preferred_element_type=F32)
        count = exps.shape[0] // 2

        def pick(tall):
            return jnp.where(low, tall[0:count], tall[count:])

        return pick(sums[:, 0:128]), pick(jnp.broadcast_to(largest, (2 * count, 128))), pick(sums[:, 128:])

    def attend(query_of, start, blocks, pairs, take):
        waiting = None
        for pair in list(pairs) + [None]:
            ready = waiting
            waiting = None if pair is None else (*scored(query_of(pair), start, blocks, pair), start, blocks, pair)
            if ready is not None:
                take(ready[-1], valued(*ready))

    def keep(pair, first, last, parts):
        for buf, value in zip((part_o, part_m, part_l), parts):
            buf[pair, first:last] = value

    def add_to(pair, parts):
        out, largest, total = parts
        old_largest = part_m[pair]
        top = jnp.maximum(largest, old_largest)
        now, before = jnp.exp(largest - top), jnp.exp(old_largest - top)
        return out * now + part_o[pair] * before, top, total * now + part_l[pair] * before

    rows = plane * tokens
    quarter = half // 2


    attend(
        lambda pair: qbuf[pair, 0], 1, half, range(PAIRS),
        lambda pair, parts: keep(pair, 0, tokens, parts),
    )

    def first_half(pairs):
        for pair in pairs:
            all_of(qbuf.at[pair], q_send.at[pair], q_recv.at[pair]).wait_recv()
        attend(
            lambda pair: qbuf[pair, 1:plane].reshape(rows - tokens, 128), 0, half, pairs,
            lambda pair, parts: keep(pair, tokens, rows, parts),
        )

    first_half(range(0, 2))
    first_half(range(2, PAIRS))
    need(half, half + quarter, pairs_all)

    def all_queries(pair):
        return qbuf[pair].reshape(rows, 128)

    attend(
        all_queries, half + 1, quarter, range(PAIRS),
        lambda pair, parts: keep(pair, 0, rows, add_to(pair, parts)),
    )

    def all_here(pair):
        need(half + quarter, depth, [pair])
        return all_queries(pair)

    def back(pair, slot):
        return remote(
            obuf.at[pair, slot], rbuf.at[pair, slot], o_send.at[pair], o_recv.at[pair],
            in_plane(plane - slot),
        )

    def stat_back(slot):
        return remote(
            ostat_packed.at[slot], rstat_packed.at[slot], t_send, t_recv, in_plane(plane - slot)
        )

    ostat[...] = jnp.zeros_like(ostat)
    within = lax.rem(lane, HEAD_DIM)

    def send_back(pair, parts):
        out, top, total = add_to(pair, parts)
        obuf[pair] = out.astype(BF16).reshape(plane, tokens, 128)
        for slot in range(1, plane):
            back(pair, slot).start()
        stats = jnp.where(within == pair, top, ostat[...])
        ostat[...] = jnp.where(within == pair + 8, total, stats)

    attend(all_here, half + 1 + quarter, quarter, range(PAIRS), send_back)

    packs = tokens // 8
    tiles = ostat[...].reshape(plane, packs, 8, 128)
    packed = sum(
        pltpu.roll(tiles[:, pack].reshape(plane * 8, 128), 16 * pack, 1) if pack else tiles[:, pack].reshape(plane * 8, 128)
        for pack in range(packs)
    )
    ostat_packed[...] = packed.reshape(plane, 8, 128)

    @pl.loop(1, plane)
    def _(slot):
        stat_back(slot).start()

    head_lane = lax.broadcasted_iota(jnp.int32, (128, WIDTH), 0)
    feature = lax.broadcasted_iota(jnp.int32, (128, WIDTH), 1)
    from_feature = lax.rem(head_lane, HEAD_DIM) * 128 + (head_lane // HEAD_DIM) * HEAD_DIM
    spread = jnp.where((feature >= from_feature) & (feature < from_feature + HEAD_DIM), 1.0, 0.0).astype(BF16)
    rstat_packed[0] = ostat_packed[0]

    all_of(st1, s1_send, s1_recv).wait_send()
    all_of(st2, s2_send, s2_recv).wait_send()
    every = kv.at[pl.ds(0, depth - 1)]
    remote(every, every, kv_send, kv_recv.at[0, 0], in_depth(1)).wait_send()
    for pair in range(PAIRS):
        all_of(qbuf.at[pair], q_send.at[pair], q_recv.at[pair]).wait_send()

    all_of(rstat_packed, t_send, t_recv).wait_recv()
    packed = rstat_packed[...].reshape(plane * 8, 128)
    tiles = [pltpu.roll(packed, 128 - 16 * pack, 1) if pack else packed for pack in range(packs)]
    stats = jnp.concatenate([tile.reshape(plane, 8, 128) for tile in tiles], axis=1)
    largest = jnp.max(stats, axis=0, keepdims=True)
    used = within < PAIRS
    weights = jnp.where(used, jnp.exp(stats - largest), 0.0)
    sums = pltpu.roll(stats.reshape(rows, 128), 120, 1).reshape(plane, tokens, 128)
    totals = jnp.where(used, jnp.sum(weights * sums, axis=0, keepdims=True), 1.0)
    shares = (weights / totals).reshape(rows, 128)
    upper = shares.astype(BF16)
    lower = (shares - upper.astype(F32)).astype(BF16)
    flat = jnp.dot(upper, spread, preferred_element_type=F32) + jnp.dot(lower, spread, preferred_element_type=F32)

    for pair in range(PAIRS):
        all_of(rbuf.at[pair], o_send.at[pair], o_recv.at[pair]).wait_recv()
        cols = slice(pair * 128, (pair + 1) * 128)
        scale = flat[:, cols].reshape(plane, tokens, 128)
        part = obuf[pair, 0].astype(F32) * scale[0]
        part = part + jnp.sum(rbuf[pair, 1:plane].astype(F32) * scale[1:], axis=0)
        result[0, :, cols] = part.astype(BF16)

    for pair in range(PAIRS):
        all_of(obuf.at[pair], o_send.at[pair], o_recv.at[pair]).wait_send()
    all_of(ostat_packed, t_send, t_recv).wait_send()


def hand_over(result, att, fresh_keys, fresh_values, sems):
    copies = [
        pltpu.make_async_copy(result.at[i], out, sems.at[i])
        for i, out in enumerate((att, fresh_keys, fresh_values))
    ]
    for copy in copies:
        copy.start()
    for copy in copies:
        copy.wait()


def on_device(plane, x, gain, bias, wq, wk, wv, k, v):
    depth = lax.axis_size("rows") // plane
    tokens = x.shape[0]
    rows = plane * tokens
    dma = pltpu.SemaphoreType.DMA
    anywhere = pl.BlockSpec(memory_space=pltpu.HBM)
    local = pl.BlockSpec(memory_space=pltpu.VMEM)
    out = jax.ShapeDtypeStruct((tokens, WIDTH), BF16)
    result = pl.pallas_call(
        functools.partial(kernel, depth, plane, tokens),
        out_shape=pltpu.VMEM((3, tokens, WIDTH), BF16),
        in_specs=[anywhere, local, local] + [anywhere] * 5,
        out_specs=local,
        scratch_shapes=[
            pltpu.VMEM((tokens, CHANNELS), BF16),
            pltpu.VMEM((depth + 1, PAIRS, 2, tokens, 128), BF16),
            pltpu.VMEM((CHANNELS, WIDTH), BF16),
            pltpu.VMEM((CHANNELS, WIDTH), BF16),
            pltpu.VMEM((CHANNELS, WIDTH), BF16),
            pltpu.VMEM((CHANNELS, 128), BF16),
            pltpu.VMEM((PAIRS, plane, tokens, 128), BF16),
            pltpu.VMEM((plane, 2, 128), F32),
            pltpu.VMEM((depth, 2, 128), F32),
            pltpu.VMEM((PAIRS, rows, 128), F32),
            pltpu.VMEM((PAIRS, rows, 128), F32),
            pltpu.VMEM((PAIRS, rows, 128), F32),
            pltpu.VMEM((PAIRS, plane, tokens, 128), BF16),
            pltpu.VMEM((PAIRS, plane, tokens, 128), BF16),
            pltpu.VMEM((rows, 128), F32),
            pltpu.VMEM((plane, 8, 128), F32),
            pltpu.VMEM((plane, 8, 128), F32),
            dma((4,)), dma((PAIRS, 2)),
            dma, dma, dma, dma,
            dma((PAIRS,)), dma((PAIRS,)),
            dma, dma((depth + 1, PAIRS)),
            dma((PAIRS,)), dma((PAIRS,)),
            dma, dma,
        ],
        compiler_params=pltpu.CompilerParams(
            collective_id=0, has_side_effects=True, vmem_limit_bytes=60 * 1024 * 1024
        ),
        name="attention_of_plane",
    )(x, gain, bias, wq, wk, wv, k, v)
    return pl.pallas_call(
        hand_over,
        out_shape=(out, out, out),
        in_specs=[local],
        out_specs=(anywhere,) * 3,
        scratch_shapes=[dma((3,))],
        name="hand_over",
    )(pltpu.with_memory_space_constraint(result, pltpu.VMEM))


def solution(mesh, plane=PLANE):
    split = P(("batch", "rows"), None)
    return jax.shard_map(
        functools.partial(on_device, plane),
        mesh=mesh,
        in_specs=(split, P(), P(), P(), P(), P(), split, split),
        out_specs=(split, split, split),
        check_vma=False,
    )
```

```python
import functools

import jax
import jax.numpy as jnp
from jax import lax
from jax.experimental import pallas as pl
from jax.experimental.pallas import tpu as pltpu
from jax.sharding import PartitionSpec as P

CHANNELS = 1280
GROUPS = 32
GROUP_WIDTH = CHANNELS // GROUPS
HEADS = 10
HEAD_DIM = 64
WIDTH = HEADS * HEAD_DIM
PAIRS = HEADS // 2
EPSILON = 1e-05
PLANE = 8

F32 = jnp.float32
BF16 = jnp.bfloat16
MESH = pl.DeviceIdType.MESH
NT = (((1,), (1,)), ((), ()))


def exact_dot(value, right, dims):
    first = value.astype(BF16).astype(F32)
    second = (value - first).astype(BF16).astype(F32)
    terms = jnp.concatenate([first, second, value - first - second], axis=0).astype(BF16)
    out = lax.dot_general(terms, right, dims, preferred_element_type=F32)
    return out[0:8] + out[8:16] + out[16:24]


def to_groups(value, member):
    return exact_dot(value, member, (((1,), (0,)), ((), ())))


def to_channels(value, member):
    return exact_dot(value, member, NT)


def kernel(
    depth, plane, tokens,
    x_in, gain, bias, wq_in, wk_in, wv_in, k_in, v_in,
    result,
    xbuf, kv, wq, wk, wv, member, nbuf, qbuf, st1, st2,
    part_o, part_m, part_l, obuf, rbuf, ostat, ostat_packed, rstat_packed,
    in_sem, kv_sem, s1_send, s1_recv, s2_send, s2_recv, x_send, x_recv,
    kv_send, kv_recv, o_send, o_recv, t_send, t_recv,
):
    row = lax.axis_index("rows")
    z, p = row // plane, lax.rem(row, plane)
    half = depth // 2

    def in_plane(step):
        return {"rows": z * plane + lax.rem(p + step, plane)}

    def in_depth(step):
        return {"rows": lax.rem(z + step, depth) * plane + p}

    def remote(src, dst, send, recv, device):
        return pltpu.make_async_remote_copy(
            src_ref=src, dst_ref=dst, send_sem=send, recv_sem=recv,
            device_id=device, device_id_type=MESH,
        )

    barrier = pltpu.get_barrier_semaphore()

    @pl.loop(1, depth)
    def _(step):
        pl.semaphore_signal(barrier, inc=1, device_id=in_depth(step), device_id_type=MESH)

    @pl.loop(1, plane)
    def _(step):
        pl.semaphore_signal(barrier, inc=1, device_id=in_plane(step), device_id_type=MESH)

    blocks_in = [
        pltpu.make_async_copy(src.at[:, pl.ds(pair * 128, 128)], kv.at[0, pair, kind], kv_sem.at[pair, kind])
        for pair in range(PAIRS)
        for kind, src in enumerate((k_in, v_in))
    ]
    loads = [
        pltpu.make_async_copy(src, dst, in_sem.at[i])
        for i, (src, dst) in enumerate([(x_in, xbuf.at[0]), (wq_in, wq), (wk_in, wk), (wv_in, wv)])
    ]
    for load in blocks_in + loads:
        load.start()

    channel = lax.broadcasted_iota(jnp.int32, (CHANNELS, 128), 0)
    group = lax.broadcasted_iota(jnp.int32, (CHANNELS, 128), 1)
    first = group * GROUP_WIDTH
    inside = (channel >= first) & (channel < first + GROUP_WIDTH) & (group < GROUPS)
    member[...] = jnp.where(inside, 1.0, 0.0).astype(BF16)

    for load in blocks_in:
        load.wait()
    pl.semaphore_wait(barrier, plane + depth - 2)

    def stat1(step):
        return remote(st1.at[0], st1.at[step], s1_send, s1_recv, in_plane(step))

    def stat2(step):
        return remote(st2.at[0], st2.at[step], s2_send, s2_recv, in_depth(step))

    def share(step):
        return remote(xbuf.at[0], xbuf.at[step], x_send, x_recv, in_plane(step))

    def all_of(buf, send, recv):
        rest = buf.at[pl.ds(1, buf.shape[0] - 1)]
        return remote(rest, rest, send, recv, in_plane(1))

    order = [0]
    for step in range(1, half):
        order += [step, depth - step]
    order += [half]
    middle = half
    place = {block: at if at < middle else at + 1 for at, block in enumerate(order)}

    def hop(way, pair, distance):
        before = distance - 1 if distance % 2 else distance - 2
        ends = [at if way == 0 else (depth - at) % depth for at in (before, distance)]
        by = distance - before if way == 0 else depth - (distance - before)
        here, there = place[ends[0]], place[ends[1]]
        return remote(kv.at[here, pair], kv.at[there, pair], kv_send, kv_recv.at[there, pair], in_depth(by))

    def length(way, pair):
        return half if pair % 2 == way else half - 1

    both_ways = (0, 1)
    pairs_all = range(PAIRS)
    seen = {(0, pair) for pair in pairs_all}

    def arrive(distance, pair):
        if (distance, pair) not in seen:
            seen.add((distance, pair))
            for way in both_ways:
                if distance <= length(way, pair):
                    hop(way, pair, distance).wait_recv()

    def need(first, last, pairs):
        for pair in pairs:
            for distance in sorted(min(block, depth - block) for block in order[first:last]):
                arrive(distance, pair)

    def forward(stop, pairs, hops=(2, 1)):
        if stop >= half:
            return
        for by in hops:
            for pair in pairs:
                arrive(stop, pair)
                for way in both_ways:
                    if stop + by <= length(way, pair):
                        hop(way, pair, stop + by).start()

    def merged(stats):
        means, spread = stats[:, 0, :], stats[:, 1, :]
        mean = jnp.mean(means, axis=0, keepdims=True)
        apart = means - mean
        return mean, jnp.mean(spread + apart * apart, axis=0, keepdims=True)

    forward(0, pairs_all, (2,))
    loads[0].wait()
    for step in range(1, plane):
        share(step).start()

    x = xbuf[0]
    count = tokens * GROUP_WIDTH
    mean = jnp.sum(jnp.dot(x, member[...], preferred_element_type=F32), axis=0, keepdims=True) / count
    centered = x.astype(F32) - to_channels(jnp.broadcast_to(mean, (8, 128)), member[...])[0:1]
    squares = jnp.sum((centered * centered).reshape(tokens // 8, 8, CHANNELS), axis=0)
    var = jnp.sum(to_groups(squares, member[...]), axis=0, keepdims=True) / count
    st1[0, 0:1, :] = mean
    st1[0, 1:2, :] = var

    @pl.loop(1, plane)
    def _(step):
        stat1(step).start()

    forward(0, pairs_all, (1,))
    forward(2, range(0, 2))
    all_of(st1, s1_send, s1_recv).wait_recv()

    mean, var = merged(st1[...])
    st2[0, 0:1, :] = mean
    st2[0, 1:2, :] = var

    @pl.loop(1, depth)
    def _(step):
        stat2(step).start()

    forward(2, range(2, PAIRS))
    forward(4, range(0, 3))
    all_of(st2, s2_send, s2_recv).wait_recv()

    mean, var = merged(st2[...])
    forward(4, range(3, PAIRS))
    line = lax.broadcasted_iota(jnp.int32, (8, 128), 0)
    wide = to_channels(jnp.where(line == 0, mean, lax.rsqrt(var + EPSILON)), member[...])
    mean_chan = wide[0:1]
    scale_chan = wide[1:2] * gain[...].reshape(1, CHANNELS)
    bias_chan = bias[...].reshape(1, CHANNELS)

    def normalised(block):
        return ((block.astype(F32) - mean_chan) * scale_chan + bias_chan).astype(BF16)

    own = normalised(xbuf[0])
    nbuf[0] = own
    for kind, load in ((0, loads[2]), (1, loads[3])):
        load.wait()
        fresh = jnp.dot(own, (wk, wv)[kind][...], preferred_element_type=F32).astype(BF16)
        for pair in pairs_all:
            kv[middle, pair, kind] = fresh[:, pair * 128 : (pair + 1) * 128]
        result[1 + kind] = fresh
    forward(6, range(0, 3))
    loads[1].wait()
    all_of(xbuf, x_send, x_recv).wait_recv()

    @pl.loop(1, plane)
    def _(slot):
        nbuf[slot] = normalised(xbuf[slot])

    rows = plane * tokens
    normed = nbuf[...].reshape(rows, CHANNELS)
    for start in range(0, WIDTH, 256):
        end = min(start + 256, WIDTH)
        query = jnp.dot(normed, wq[:, start:end], preferred_element_type=F32).astype(BF16)
        query = query * jnp.asarray(HEAD_DIM**-0.5, BF16)
        for pair in range(start // 128, end // 128):
            at = pair * 128 - start
            qbuf[pair] = query[:, at : at + 128]
    forward(6, range(3, PAIRS))

    lane = lax.broadcasted_iota(jnp.int32, (1, 128), 1)
    low = lane < HEAD_DIM
    masks = (jnp.where(low, 1.0, 0.0).astype(BF16), jnp.where(low, 0.0, 1.0).astype(BF16))

    def gathered(kind, start, blocks, pair):
        return kv[start : start + blocks, pair, kind].reshape(blocks * tokens, 128)

    def scored(query, start, blocks, pair):
        both = jnp.concatenate([query * masks[0], query * masks[1]], axis=0)
        keys = gathered(0, start, blocks, pair)
        scores = lax.dot_general(both, keys, NT, preferred_element_type=F32)
        largest = jnp.max(scores, axis=-1, keepdims=True)
        return jnp.exp(scores - largest).astype(BF16), largest

    def valued(exps, largest, start, blocks, pair):
        ones = jnp.ones((blocks * tokens, 128), BF16)
        right = jnp.concatenate([gathered(1, start, blocks, pair), ones], axis=1)
        sums = jnp.dot(exps, right, preferred_element_type=F32)
        count = exps.shape[0] // 2

        def pick(tall):
            return jnp.where(low, tall[0:count], tall[count:])

        return pick(sums[:, 0:128]), pick(jnp.broadcast_to(largest, (2 * count, 128))), pick(sums[:, 128:])

    def attend(query_of, start, blocks, pairs, take):
        waiting = None
        for pair in list(pairs) + [None]:
            ready = waiting
            waiting = None if pair is None else (*scored(query_of(pair), start, blocks, pair), start, blocks, pair)
            if ready is not None:
                take(ready[-1], valued(*ready))

    def keep(pair, first, last, parts):
        for buf, value in zip((part_o, part_m, part_l), parts):
            buf[pair, first:last] = value

    def add_to(pair, parts):
        out, largest, total = parts
        old_largest = part_m[pair]
        top = jnp.maximum(largest, old_largest)
        now, before = jnp.exp(largest - top), jnp.exp(old_largest - top)
        return out * now + part_o[pair] * before, top, total * now + part_l[pair] * before

    need(0, half, pairs_all)
    attend(
        lambda pair: qbuf[pair, 0:tokens], 1, half, pairs_all,
        lambda pair, parts: keep(pair, 0, tokens, parts),
    )
    attend(
        lambda pair: qbuf[pair, tokens:rows], 0, half, pairs_all,
        lambda pair, parts: keep(pair, tokens, rows, parts),
    )

    def all_here(pair):
        need(half, depth, [pair])
        return qbuf[pair]

    def back(pair, slot):
        return remote(
            obuf.at[pair, slot], rbuf.at[pair, slot], o_send.at[pair], o_recv.at[pair],
            in_plane(plane - slot),
        )

    def stat_back(slot):
        return remote(
            ostat_packed.at[slot], rstat_packed.at[slot], t_send, t_recv, in_plane(plane - slot)
        )

    ostat[...] = jnp.zeros_like(ostat)
    within = lax.rem(lane, HEAD_DIM)

    def send_back(pair, parts):
        out, top, total = add_to(pair, parts)
        obuf[pair] = out.astype(BF16).reshape(plane, tokens, 128)
        for slot in range(1, plane):
            back(pair, slot).start()
        stats = jnp.where(within == pair, top, ostat[...])
        ostat[...] = jnp.where(within == pair + 8, total, stats)

    attend(all_here, half + 1, half, pairs_all, send_back)

    packs = tokens // 8
    tiles = ostat[...].reshape(plane, packs, 8, 128)
    packed = sum(
        pltpu.roll(tiles[:, pack].reshape(plane * 8, 128), 16 * pack, 1) if pack else tiles[:, pack].reshape(plane * 8, 128)
        for pack in range(packs)
    )
    ostat_packed[...] = packed.reshape(plane, 8, 128)

    @pl.loop(1, plane)
    def _(slot):
        stat_back(slot).start()

    head_lane = lax.broadcasted_iota(jnp.int32, (128, WIDTH), 0)
    feature = lax.broadcasted_iota(jnp.int32, (128, WIDTH), 1)
    from_feature = lax.rem(head_lane, HEAD_DIM) * 128 + (head_lane // HEAD_DIM) * HEAD_DIM
    spread = jnp.where((feature >= from_feature) & (feature < from_feature + HEAD_DIM), 1.0, 0.0).astype(BF16)
    rstat_packed[0] = ostat_packed[0]

    all_of(st1, s1_send, s1_recv).wait_send()
    all_of(st2, s2_send, s2_recv).wait_send()
    every = kv.at[pl.ds(0, depth - 1)]
    remote(every, every, kv_send, kv_recv.at[0, 0], in_depth(1)).wait_send()
    all_of(xbuf, x_send, x_recv).wait_send()

    all_of(rstat_packed, t_send, t_recv).wait_recv()
    packed = rstat_packed[...].reshape(plane * 8, 128)
    tiles = [pltpu.roll(packed, 128 - 16 * pack, 1) if pack else packed for pack in range(packs)]
    stats = jnp.concatenate([tile.reshape(plane, 8, 128) for tile in tiles], axis=1)
    largest = jnp.max(stats, axis=0, keepdims=True)
    used = within < PAIRS
    weights = jnp.where(used, jnp.exp(stats - largest), 0.0)
    sums = pltpu.roll(stats.reshape(rows, 128), 120, 1).reshape(plane, tokens, 128)
    totals = jnp.where(used, jnp.sum(weights * sums, axis=0, keepdims=True), 1.0)
    shares = (weights / totals).reshape(rows, 128)
    upper = shares.astype(BF16)
    lower = (shares - upper.astype(F32)).astype(BF16)
    flat = jnp.dot(upper, spread, preferred_element_type=F32) + jnp.dot(lower, spread, preferred_element_type=F32)

    for pair in range(PAIRS):
        all_of(rbuf.at[pair], o_send.at[pair], o_recv.at[pair]).wait_recv()
        cols = slice(pair * 128, (pair + 1) * 128)
        scale = flat[:, cols].reshape(plane, tokens, 128)
        part = obuf[pair, 0].astype(F32) * scale[0]
        part = part + jnp.sum(rbuf[pair, 1:plane].astype(F32) * scale[1:], axis=0)
        result[0, :, cols] = part.astype(BF16)

    for pair in range(PAIRS):
        all_of(obuf.at[pair], o_send.at[pair], o_recv.at[pair]).wait_send()
    all_of(ostat_packed, t_send, t_recv).wait_send()


def hand_over(result, att, fresh_keys, fresh_values, sems):
    copies = [
        pltpu.make_async_copy(result.at[i], out, sems.at[i])
        for i, out in enumerate((att, fresh_keys, fresh_values))
    ]
    for copy in copies:
        copy.start()
    for copy in copies:
        copy.wait()


def on_device(plane, x, gain, bias, wq, wk, wv, k, v):
    depth = lax.axis_size("rows") // plane
    tokens = x.shape[0]
    rows = plane * tokens
    dma = pltpu.SemaphoreType.DMA
    anywhere = pl.BlockSpec(memory_space=pltpu.HBM)
    local = pl.BlockSpec(memory_space=pltpu.VMEM)
    out = jax.ShapeDtypeStruct((tokens, WIDTH), BF16)
    result = pl.pallas_call(
        functools.partial(kernel, depth, plane, tokens),
        out_shape=pltpu.VMEM((3, tokens, WIDTH), BF16),
        in_specs=[anywhere, local, local] + [anywhere] * 5,
        out_specs=local,
        scratch_shapes=[
            pltpu.VMEM((plane, tokens, CHANNELS), BF16),
            pltpu.VMEM((depth + 1, PAIRS, 2, tokens, 128), BF16),
            pltpu.VMEM((CHANNELS, WIDTH), BF16),
            pltpu.VMEM((CHANNELS, WIDTH), BF16),
            pltpu.VMEM((CHANNELS, WIDTH), BF16),
            pltpu.VMEM((CHANNELS, 128), BF16),
            pltpu.VMEM((plane, tokens, CHANNELS), BF16),
            pltpu.VMEM((PAIRS, rows, 128), BF16),
            pltpu.VMEM((plane, 2, 128), F32),
            pltpu.VMEM((depth, 2, 128), F32),
            pltpu.VMEM((PAIRS, rows, 128), F32),
            pltpu.VMEM((PAIRS, rows, 128), F32),
            pltpu.VMEM((PAIRS, rows, 128), F32),
            pltpu.VMEM((PAIRS, plane, tokens, 128), BF16),
            pltpu.VMEM((PAIRS, plane, tokens, 128), BF16),
            pltpu.VMEM((rows, 128), F32),
            pltpu.VMEM((plane, 8, 128), F32),
            pltpu.VMEM((plane, 8, 128), F32),
            dma((4,)), dma((PAIRS, 2)),
            dma, dma, dma, dma,
            dma, dma,
            dma, dma((depth + 1, PAIRS)),
            dma((PAIRS,)), dma((PAIRS,)),
            dma, dma,
        ],
        compiler_params=pltpu.CompilerParams(
            collective_id=0, has_side_effects=True, vmem_limit_bytes=60 * 1024 * 1024
        ),
        name="attention_of_plane",
    )(x, gain, bias, wq, wk, wv, k, v)
    return pl.pallas_call(
        hand_over,
        out_shape=(out, out, out),
        in_specs=[local],
        out_specs=(anywhere,) * 3,
        scratch_shapes=[dma((3,))],
        name="hand_over",
    )(pltpu.with_memory_space_constraint(result, pltpu.VMEM))


def solution(mesh, plane=PLANE):
    split = P(("batch", "rows"), None)
    return jax.shard_map(
        functools.partial(on_device, plane),
        mesh=mesh,
        in_specs=(split, P(), P(), P(), P(), P(), split, split),
        out_specs=(split, split, split),
        check_vma=False,
    )
```

```python
import functools

import jax
import jax.numpy as jnp
from jax import lax
from jax.experimental import pallas as pl
from jax.experimental.pallas import tpu as pltpu
from jax.sharding import PartitionSpec as P

CHANNELS = 1280
GROUPS = 32
GROUP_WIDTH = CHANNELS // GROUPS
HEADS = 10
HEAD_DIM = 64
WIDTH = HEADS * HEAD_DIM
PAIRS = HEADS // 2
EPSILON = 1e-05
LINE = 4
PLANE = 8

F32 = jnp.float32
BF16 = jnp.bfloat16
MESH = pl.DeviceIdType.MESH
NT = (((1,), (1,)), ((), ()))


def exact_dot(value, right, dims):
    first = value.astype(BF16).astype(F32)
    second = (value - first).astype(BF16).astype(F32)
    terms = jnp.concatenate([first, second, value - first - second], axis=0).astype(BF16)
    out = lax.dot_general(terms, right, dims, preferred_element_type=F32)
    return out[0:8] + out[8:16] + out[16:24]


def to_groups(value, member):
    return exact_dot(value, member, (((1,), (0,)), ((), ())))


def to_channels(value, member):
    return exact_dot(value, member, NT)


def kernel(
    depth, plane, tokens,
    x_in, gain, bias, wq_in, wk_in, wv_in, k_in, v_in,
    result,
    xbuf, kv, wq, wk, wv, member, nbuf, qbuf, st1, st2,
    part_o, part_m, part_l, obuf, rbuf, ostat, ostat_packed, rstat_packed,
    in_sem, kv_sem, s1_send, s1_recv, s2_send, s2_recv, x_send, x_recv,
    kv_send, kv_recv, o_send, o_recv, t_send, t_recv,
):
    row = lax.axis_index("rows")
    z, p = row // plane, lax.rem(row, plane)
    half = depth // 2

    line = min(LINE, plane)

    def in_plane(step):
        x_to = lax.rem(p // line + step // line, plane // line)
        return {"rows": z * plane + x_to * line + lax.rem(lax.rem(p, line) + step % line, line)}

    def back_in_plane(step):
        return in_plane(step // line * line + lax.rem(line - step % line, line))

    def in_depth(step):
        return {"rows": lax.rem(z + step, depth) * plane + p}

    def remote(src, dst, send, recv, device):
        return pltpu.make_async_remote_copy(
            src_ref=src, dst_ref=dst, send_sem=send, recv_sem=recv,
            device_id=device, device_id_type=MESH,
        )

    barrier = pltpu.get_barrier_semaphore()

    @pl.loop(1, depth)
    def _(step):
        pl.semaphore_signal(barrier, inc=1, device_id=in_depth(step), device_id_type=MESH)

    @pl.loop(1, plane)
    def _(step):
        pl.semaphore_signal(barrier, inc=1, device_id=in_plane(step), device_id_type=MESH)

    blocks_in = [
        pltpu.make_async_copy(src.at[:, pl.ds(pair * 128, 128)], kv.at[0, pair, kind], kv_sem.at[pair, kind])
        for pair in range(PAIRS)
        for kind, src in enumerate((k_in, v_in))
    ]
    loads = [
        pltpu.make_async_copy(src, dst, in_sem.at[i])
        for i, (src, dst) in enumerate([(x_in, xbuf.at[0]), (wq_in, wq), (wk_in, wk), (wv_in, wv)])
    ]
    for load in blocks_in + loads:
        load.start()

    channel = lax.broadcasted_iota(jnp.int32, (CHANNELS, 128), 0)
    group = lax.broadcasted_iota(jnp.int32, (CHANNELS, 128), 1)
    first = group * GROUP_WIDTH
    inside = (channel >= first) & (channel < first + GROUP_WIDTH) & (group < GROUPS)
    member[...] = jnp.where(inside, 1.0, 0.0).astype(BF16)

    for load in blocks_in:
        load.wait()
    pl.semaphore_wait(barrier, plane + depth - 2)

    def stat1(step):
        return remote(st1.at[0], st1.at[step], s1_send, s1_recv, in_plane(step))

    def stat2(step):
        return remote(st2.at[0], st2.at[step], s2_send, s2_recv, in_depth(step))

    def share(step):
        return remote(xbuf.at[0], xbuf.at[step], x_send, x_recv.at[step, 0], in_plane(step))

    def relay(side, far):
        rows = pl.ds(side * (tokens // 2), tokens // 2)
        near = far - 1 if side == 0 else far + 1
        return remote(
            xbuf.at[near, rows], xbuf.at[far, rows], x_send, x_recv.at[far, side],
            in_plane(1 if side == 0 else line - 1),
        )

    slots = range(1, plane)
    far_slots = [step for step in slots if line == 4 and step % line == 2]
    near_slots = [step for step in slots if step not in far_slots]

    def all_of(buf, send, recv):
        rest = buf.at[pl.ds(1, buf.shape[0] - 1)]
        return remote(rest, rest, send, recv, in_plane(1))

    order = [0]
    for step in range(1, half):
        order += [step, depth - step]
    order += [half]
    middle = half
    place = {block: at if at < middle else at + 1 for at, block in enumerate(order)}

    def hop(way, pair, distance):
        before = distance - 1 if distance % 2 else distance - 2
        ends = [at if way == 0 else (depth - at) % depth for at in (before, distance)]
        by = distance - before if way == 0 else depth - (distance - before)
        here, there = place[ends[0]], place[ends[1]]
        return remote(kv.at[here, pair], kv.at[there, pair], kv_send, kv_recv.at[there, pair], in_depth(by))

    def length(way, pair):
        return half if pair % 2 == way else half - 1

    both_ways = (0, 1)
    pairs_all = range(PAIRS)
    seen = {(0, pair) for pair in pairs_all}

    def arrive(distance, pair):
        if (distance, pair) not in seen:
            seen.add((distance, pair))
            for way in both_ways:
                if distance <= length(way, pair):
                    hop(way, pair, distance).wait_recv()

    def need(first, last, pairs):
        for pair in pairs:
            for distance in sorted(min(block, depth - block) for block in order[first:last]):
                arrive(distance, pair)

    def forward(stop, pairs, hops=(2, 1)):
        if stop >= half:
            return
        for by in hops:
            for pair in pairs:
                arrive(stop, pair)
                for way in both_ways:
                    if stop + by <= length(way, pair):
                        hop(way, pair, stop + by).start()

    def merged(stats):
        means, spread = stats[:, 0, :], stats[:, 1, :]
        mean = jnp.mean(means, axis=0, keepdims=True)
        apart = means - mean
        return mean, jnp.mean(spread + apart * apart, axis=0, keepdims=True)

    forward(0, pairs_all, (2,))
    loads[0].wait()
    for step in near_slots:
        share(step).start()

    x = xbuf[0]
    count = tokens * GROUP_WIDTH
    mean = jnp.sum(jnp.dot(x, member[...], preferred_element_type=F32), axis=0, keepdims=True) / count
    centered = x.astype(F32) - to_channels(jnp.broadcast_to(mean, (8, 128)), member[...])[0:1]
    squares = jnp.sum((centered * centered).reshape(tokens // 8, 8, CHANNELS), axis=0)
    var = jnp.sum(to_groups(squares, member[...]), axis=0, keepdims=True) / count
    st1[0, 0:1, :] = mean
    st1[0, 1:2, :] = var

    @pl.loop(1, plane)
    def _(step):
        stat1(step).start()

    forward(0, pairs_all, (1,))
    forward(2, range(0, 2))
    all_of(st1, s1_send, s1_recv).wait_recv()

    mean, var = merged(st1[...])
    st2[0, 0:1, :] = mean
    st2[0, 1:2, :] = var

    @pl.loop(1, depth)
    def _(step):
        stat2(step).start()

    forward(2, range(2, PAIRS))
    for step in near_slots:
        share(step).wait_recv()
    for far in far_slots:
        for side in (0, 1):
            relay(side, far).start()
    forward(4, range(0, 3))
    all_of(st2, s2_send, s2_recv).wait_recv()

    mean, var = merged(st2[...])
    forward(4, range(3, PAIRS))
    sublane = lax.broadcasted_iota(jnp.int32, (8, 128), 0)
    wide = to_channels(jnp.where(sublane == 0, mean, lax.rsqrt(var + EPSILON)), member[...])
    mean_chan = wide[0:1]
    scale_chan = wide[1:2] * gain[...].reshape(1, CHANNELS)
    bias_chan = bias[...].reshape(1, CHANNELS)

    def normalised(block):
        return ((block.astype(F32) - mean_chan) * scale_chan + bias_chan).astype(BF16)

    own = normalised(xbuf[0])
    nbuf[0] = own
    for kind, load in ((0, loads[2]), (1, loads[3])):
        load.wait()
        fresh = jnp.dot(own, (wk, wv)[kind][...], preferred_element_type=F32).astype(BF16)
        for pair in pairs_all:
            kv[middle, pair, kind] = fresh[:, pair * 128 : (pair + 1) * 128]
        result[1 + kind] = fresh
    forward(6, range(0, 3))
    loads[1].wait()
    for far in far_slots:
        for side in (0, 1):
            relay(side, far).wait_recv()

    @pl.loop(1, plane)
    def _(slot):
        nbuf[slot] = normalised(xbuf[slot])

    rows = plane * tokens
    normed = nbuf[...].reshape(rows, CHANNELS)
    for start in range(0, WIDTH, 256):
        end = min(start + 256, WIDTH)
        query = jnp.dot(normed, wq[:, start:end], preferred_element_type=F32).astype(BF16)
        query = query * jnp.asarray(HEAD_DIM**-0.5, BF16)
        for pair in range(start // 128, end // 128):
            at = pair * 128 - start
            qbuf[pair] = query[:, at : at + 128]
    forward(6, range(3, PAIRS))

    lane = lax.broadcasted_iota(jnp.int32, (1, 128), 1)
    low = lane < HEAD_DIM
    masks = (jnp.where(low, 1.0, 0.0).astype(BF16), jnp.where(low, 0.0, 1.0).astype(BF16))

    def gathered(kind, start, blocks, pair):
        return kv[start : start + blocks, pair, kind].reshape(blocks * tokens, 128)

    def scored(query, start, blocks, pair):
        both = jnp.concatenate([query * masks[0], query * masks[1]], axis=0)
        keys = gathered(0, start, blocks, pair)
        scores = lax.dot_general(both, keys, NT, preferred_element_type=F32)
        largest = jnp.max(scores, axis=-1, keepdims=True)
        return jnp.exp(scores - largest).astype(BF16), largest

    def valued(exps, largest, start, blocks, pair):
        ones = jnp.ones((blocks * tokens, 128), BF16)
        right = jnp.concatenate([gathered(1, start, blocks, pair), ones], axis=1)
        sums = jnp.dot(exps, right, preferred_element_type=F32)
        count = exps.shape[0] // 2

        def pick(tall):
            return jnp.where(low, tall[0:count], tall[count:])

        return pick(sums[:, 0:128]), pick(jnp.broadcast_to(largest, (2 * count, 128))), pick(sums[:, 128:])

    def attend(query_of, start, blocks, pairs, take):
        waiting = None
        for pair in list(pairs) + [None]:
            ready = waiting
            waiting = None if pair is None else (*scored(query_of(pair), start, blocks, pair), start, blocks, pair)
            if ready is not None:
                take(ready[-1], valued(*ready))

    def keep(pair, first, last, parts):
        for buf, value in zip((part_o, part_m, part_l), parts):
            buf[pair, first:last] = value

    def add_to(pair, parts):
        out, largest, total = parts
        old_largest = part_m[pair]
        top = jnp.maximum(largest, old_largest)
        now, before = jnp.exp(largest - top), jnp.exp(old_largest - top)
        return out * now + part_o[pair] * before, top, total * now + part_l[pair] * before

    need(0, half, pairs_all)
    attend(
        lambda pair: qbuf[pair, 0:tokens], 1, half, pairs_all,
        lambda pair, parts: keep(pair, 0, tokens, parts),
    )
    attend(
        lambda pair: qbuf[pair, tokens:rows], 0, half, pairs_all,
        lambda pair, parts: keep(pair, tokens, rows, parts),
    )

    quarter = half // 2
    need(half, half + quarter, pairs_all)
    attend(
        lambda pair: qbuf[pair], half + 1, quarter, pairs_all,
        lambda pair, parts: keep(pair, 0, rows, add_to(pair, parts)),
    )

    def all_here(pair):
        need(half + quarter, depth, [pair])
        return qbuf[pair]

    def back(pair, slot):
        return remote(
            obuf.at[pair, slot], rbuf.at[pair, slot], o_send.at[pair], o_recv.at[pair],
            back_in_plane(slot),
        )

    def stat_back(slot):
        return remote(
            ostat_packed.at[slot], rstat_packed.at[slot], t_send, t_recv, back_in_plane(slot)
        )

    ostat[...] = jnp.zeros_like(ostat)
    within = lax.rem(lane, HEAD_DIM)

    def send_back(pair, parts):
        out, top, total = add_to(pair, parts)
        obuf[pair] = out.astype(BF16).reshape(plane, tokens, 128)
        for slot in range(1, plane):
            back(pair, slot).start()
        stats = jnp.where(within == pair, top, ostat[...])
        ostat[...] = jnp.where(within == pair + 8, total, stats)

    attend(all_here, half + 1 + quarter, quarter, pairs_all, send_back)

    packs = tokens // 8
    tiles = ostat[...].reshape(plane, packs, 8, 128)
    packed = sum(
        pltpu.roll(tiles[:, pack].reshape(plane * 8, 128), 16 * pack, 1) if pack else tiles[:, pack].reshape(plane * 8, 128)
        for pack in range(packs)
    )
    ostat_packed[...] = packed.reshape(plane, 8, 128)

    @pl.loop(1, plane)
    def _(slot):
        stat_back(slot).start()

    head_lane = lax.broadcasted_iota(jnp.int32, (128, WIDTH), 0)
    feature = lax.broadcasted_iota(jnp.int32, (128, WIDTH), 1)
    from_feature = lax.rem(head_lane, HEAD_DIM) * 128 + (head_lane // HEAD_DIM) * HEAD_DIM
    spread = jnp.where((feature >= from_feature) & (feature < from_feature + HEAD_DIM), 1.0, 0.0).astype(BF16)
    rstat_packed[0] = ostat_packed[0]

    all_of(st1, s1_send, s1_recv).wait_send()
    all_of(st2, s2_send, s2_recv).wait_send()
    every = kv.at[pl.ds(0, depth - 1)]
    remote(every, every, kv_send, kv_recv.at[0, 0], in_depth(1)).wait_send()
    all_of(xbuf, x_send, x_recv.at[0, 0]).wait_send()

    all_of(rstat_packed, t_send, t_recv).wait_recv()
    packed = rstat_packed[...].reshape(plane * 8, 128)
    tiles = [pltpu.roll(packed, 128 - 16 * pack, 1) if pack else packed for pack in range(packs)]
    stats = jnp.concatenate([tile.reshape(plane, 8, 128) for tile in tiles], axis=1)
    largest = jnp.max(stats, axis=0, keepdims=True)
    used = within < PAIRS
    weights = jnp.where(used, jnp.exp(stats - largest), 0.0)
    sums = pltpu.roll(stats.reshape(rows, 128), 120, 1).reshape(plane, tokens, 128)
    totals = jnp.where(used, jnp.sum(weights * sums, axis=0, keepdims=True), 1.0)
    shares = (weights / totals).reshape(rows, 128)
    upper = shares.astype(BF16)
    lower = (shares - upper.astype(F32)).astype(BF16)
    flat = jnp.dot(upper, spread, preferred_element_type=F32) + jnp.dot(lower, spread, preferred_element_type=F32)

    for pair in range(PAIRS):
        all_of(rbuf.at[pair], o_send.at[pair], o_recv.at[pair]).wait_recv()
        cols = slice(pair * 128, (pair + 1) * 128)
        scale = flat[:, cols].reshape(plane, tokens, 128)
        part = obuf[pair, 0].astype(F32) * scale[0]
        part = part + jnp.sum(rbuf[pair, 1:plane].astype(F32) * scale[1:], axis=0)
        result[0, :, cols] = part.astype(BF16)

    for pair in range(PAIRS):
        all_of(obuf.at[pair], o_send.at[pair], o_recv.at[pair]).wait_send()
    all_of(ostat_packed, t_send, t_recv).wait_send()


def hand_over(result, att, fresh_keys, fresh_values, sems):
    copies = [
        pltpu.make_async_copy(result.at[i], out, sems.at[i])
        for i, out in enumerate((att, fresh_keys, fresh_values))
    ]
    for copy in copies:
        copy.start()
    for copy in copies:
        copy.wait()


def on_device(plane, x, gain, bias, wq, wk, wv, k, v):
    depth = lax.axis_size("rows") // plane
    tokens = x.shape[0]
    rows = plane * tokens
    dma = pltpu.SemaphoreType.DMA
    anywhere = pl.BlockSpec(memory_space=pltpu.HBM)
    local = pl.BlockSpec(memory_space=pltpu.VMEM)
    out = jax.ShapeDtypeStruct((tokens, WIDTH), BF16)
    result = pl.pallas_call(
        functools.partial(kernel, depth, plane, tokens),
        out_shape=pltpu.VMEM((3, tokens, WIDTH), BF16),
        in_specs=[anywhere, local, local] + [anywhere] * 5,
        out_specs=local,
        scratch_shapes=[
            pltpu.VMEM((plane, tokens, CHANNELS), BF16),
            pltpu.VMEM((depth + 1, PAIRS, 2, tokens, 128), BF16),
            pltpu.VMEM((CHANNELS, WIDTH), BF16),
            pltpu.VMEM((CHANNELS, WIDTH), BF16),
            pltpu.VMEM((CHANNELS, WIDTH), BF16),
            pltpu.VMEM((CHANNELS, 128), BF16),
            pltpu.VMEM((plane, tokens, CHANNELS), BF16),
            pltpu.VMEM((PAIRS, rows, 128), BF16),
            pltpu.VMEM((plane, 2, 128), F32),
            pltpu.VMEM((depth, 2, 128), F32),
            pltpu.VMEM((PAIRS, rows, 128), F32),
            pltpu.VMEM((PAIRS, rows, 128), F32),
            pltpu.VMEM((PAIRS, rows, 128), F32),
            pltpu.VMEM((PAIRS, plane, tokens, 128), BF16),
            pltpu.VMEM((PAIRS, plane, tokens, 128), BF16),
            pltpu.VMEM((rows, 128), F32),
            pltpu.VMEM((plane, 8, 128), F32),
            pltpu.VMEM((plane, 8, 128), F32),
            dma((4,)), dma((PAIRS, 2)),
            dma, dma, dma, dma,
            dma, dma((plane, 2)),
            dma, dma((depth + 1, PAIRS)),
            dma((PAIRS,)), dma((PAIRS,)),
            dma, dma,
        ],
        compiler_params=pltpu.CompilerParams(
            collective_id=0, has_side_effects=True, vmem_limit_bytes=60 * 1024 * 1024
        ),
        name="attention_of_plane",
    )(x, gain, bias, wq, wk, wv, k, v)
    return pl.pallas_call(
        hand_over,
        out_shape=(out, out, out),
        in_specs=[local],
        out_specs=(anywhere,) * 3,
        scratch_shapes=[dma((3,))],
        name="hand_over",
    )(pltpu.with_memory_space_constraint(result, pltpu.VMEM))


def solution(mesh, plane=PLANE):
    split = P(("batch", "rows"), None)
    return jax.shard_map(
        functools.partial(on_device, plane),
        mesh=mesh,
        in_specs=(split, P(), P(), P(), P(), P(), split, split),
        out_specs=(split, split, split),
        check_vma=False,
    )
```

```python
import functools

import jax
import jax.numpy as jnp
from jax import lax
from jax.experimental import pallas as pl
from jax.experimental.pallas import tpu as pltpu
from jax.sharding import PartitionSpec as P

CHANNELS = 1280
GROUPS = 32
GROUP_WIDTH = CHANNELS // GROUPS
HEADS = 10
HEAD_DIM = 64
WIDTH = HEADS * HEAD_DIM
PAIRS = HEADS // 2
EPSILON = 1e-05
LINE = 4
SKIPPED = 4
PLANE = 8

F32 = jnp.float32
BF16 = jnp.bfloat16
MESH = pl.DeviceIdType.MESH
NT = (((1,), (1,)), ((), ()))


def exact_dot(value, right, dims):
    first = value.astype(BF16).astype(F32)
    second = (value - first).astype(BF16).astype(F32)
    terms = jnp.concatenate([first, second, value - first - second], axis=0).astype(BF16)
    out = lax.dot_general(terms, right, dims, preferred_element_type=F32)
    return out[0:8] + out[8:16] + out[16:24]


def to_groups(value, member):
    return exact_dot(value, member, (((1,), (0,)), ((), ())))


def to_channels(value, member):
    return exact_dot(value, member, NT)


def kernel(
    depth, plane, tokens,
    x_in, gain, bias, wq_in, wk_in, wv_in, k_in, v_in,
    result,
    xbuf, kv, wq, wk, wv, member, nbuf, qbuf, st1, st2,
    part_o, part_m, part_l, obuf, rbuf, ostat, ostat_packed, rstat_packed,
    in_sem, kv_sem, s1_send, s1_recv, s2_send, s2_recv, x_send, x_recv,
    kv_send, kv_recv, o_send, o_recv, t_send, t_recv,
):
    row = lax.axis_index("rows")
    z, p = row // plane, lax.rem(row, plane)
    half = depth // 2

    line = min(LINE, plane)

    def in_plane(step):
        x_to = lax.rem(p // line + step // line, plane // line)
        return {"rows": z * plane + x_to * line + lax.rem(lax.rem(p, line) + step % line, line)}

    def back_in_plane(step):
        return in_plane(step // line * line + lax.rem(line - step % line, line))

    def in_depth(step):
        return {"rows": lax.rem(z + step, depth) * plane + p}

    def remote(src, dst, send, recv, device):
        return pltpu.make_async_remote_copy(
            src_ref=src, dst_ref=dst, send_sem=send, recv_sem=recv,
            device_id=device, device_id_type=MESH,
        )

    barrier = pltpu.get_barrier_semaphore()

    @pl.loop(1, depth)
    def _(step):
        pl.semaphore_signal(barrier, inc=1, device_id=in_depth(step), device_id_type=MESH)

    @pl.loop(1, plane)
    def _(step):
        pl.semaphore_signal(barrier, inc=1, device_id=in_plane(step), device_id_type=MESH)

    blocks_in = [
        pltpu.make_async_copy(src.at[:, pl.ds(pair * 128, 128)], kv.at[0, pair, kind], kv_sem.at[pair, kind])
        for pair in range(PAIRS)
        for kind, src in enumerate((k_in, v_in))
    ]
    loads = [
        pltpu.make_async_copy(src, dst, in_sem.at[i])
        for i, (src, dst) in enumerate([(x_in, xbuf.at[0]), (wq_in, wq), (wk_in, wk), (wv_in, wv)])
    ]
    for load in blocks_in + loads:
        load.start()

    channel = lax.broadcasted_iota(jnp.int32, (CHANNELS, 128), 0)
    group = lax.broadcasted_iota(jnp.int32, (CHANNELS, 128), 1)
    first = group * GROUP_WIDTH
    inside = (channel >= first) & (channel < first + GROUP_WIDTH) & (group < GROUPS)
    member[...] = jnp.where(inside, 1.0, 0.0).astype(BF16)

    for load in blocks_in:
        load.wait()
    pl.semaphore_wait(barrier, plane + depth - 2)

    def stat1(step):
        return remote(st1.at[0], st1.at[step], s1_send, s1_recv, in_plane(step))

    def stat2(step):
        return remote(st2.at[0], st2.at[step], s2_send, s2_recv, in_depth(step))

    def share(step):
        return remote(xbuf.at[0], xbuf.at[step], x_send, x_recv.at[step, 0], in_plane(step))

    def relay(side, far):
        rows = pl.ds(side * (tokens // 2), tokens // 2)
        near = far - 1 if side == 0 else far + 1
        return remote(
            xbuf.at[near, rows], xbuf.at[far, rows], x_send, x_recv.at[far, side],
            in_plane(1 if side == 0 else line - 1),
        )

    slots = range(1, plane)
    far_slots = [step for step in slots if line == 4 and step % line == 2]
    near_slots = [step for step in slots if step not in far_slots]

    def all_of(buf, send, recv):
        rest = buf.at[pl.ds(1, buf.shape[0] - 1)]
        return remote(rest, rest, send, recv, in_plane(1))

    order = [0]
    for step in range(1, half):
        order += [step, depth - step]
    order += [half]
    middle = half
    place = {block: at if at < middle else at + 1 for at, block in enumerate(order)}

    def hop(way, pair, distance):
        before = distance - 2 if distance % 2 == 0 and distance <= SKIPPED else distance - 1
        ends = [at if way == 0 else (depth - at) % depth for at in (before, distance)]
        by = distance - before if way == 0 else depth - (distance - before)
        here, there = place[ends[0]], place[ends[1]]
        return remote(kv.at[here, pair], kv.at[there, pair], kv_send, kv_recv.at[there, pair], in_depth(by))

    def length(way, pair):
        return half if pair % 2 == way else half - 1

    both_ways = (0, 1)
    pairs_all = range(PAIRS)
    seen = {(0, pair) for pair in pairs_all}

    def arrive(distance, pair):
        if (distance, pair) not in seen:
            seen.add((distance, pair))
            for way in both_ways:
                if distance <= length(way, pair):
                    hop(way, pair, distance).wait_recv()

    def need(first, last, pairs):
        for pair in pairs:
            for distance in sorted(min(block, depth - block) for block in order[first:last]):
                arrive(distance, pair)

    def forward(stop, pairs, hops=(2, 1)):
        if stop >= half:
            return
        for by in hops if stop < SKIPPED else (1,):
            for pair in pairs:
                arrive(stop, pair)
                for way in both_ways:
                    if stop + by <= length(way, pair):
                        hop(way, pair, stop + by).start()

    def merged(stats):
        means, spread = stats[:, 0, :], stats[:, 1, :]
        mean = jnp.mean(means, axis=0, keepdims=True)
        apart = means - mean
        return mean, jnp.mean(spread + apart * apart, axis=0, keepdims=True)

    forward(0, pairs_all, (2,))
    loads[0].wait()
    for step in near_slots:
        share(step).start()

    x = xbuf[0]
    count = tokens * GROUP_WIDTH
    mean = jnp.sum(jnp.dot(x, member[...], preferred_element_type=F32), axis=0, keepdims=True) / count
    centered = x.astype(F32) - to_channels(jnp.broadcast_to(mean, (8, 128)), member[...])[0:1]
    squares = jnp.sum((centered * centered).reshape(tokens // 8, 8, CHANNELS), axis=0)
    var = jnp.sum(to_groups(squares, member[...]), axis=0, keepdims=True) / count
    st1[0, 0:1, :] = mean
    st1[0, 1:2, :] = var

    @pl.loop(1, plane)
    def _(step):
        stat1(step).start()

    forward(0, pairs_all, (1,))
    forward(2, range(0, 2))
    all_of(st1, s1_send, s1_recv).wait_recv()

    mean, var = merged(st1[...])
    st2[0, 0:1, :] = mean
    st2[0, 1:2, :] = var

    @pl.loop(1, depth)
    def _(step):
        stat2(step).start()

    forward(2, range(2, PAIRS))
    for step in near_slots:
        share(step).wait_recv()
    for far in far_slots:
        for side in (0, 1):
            relay(side, far).start()
    forward(4, pairs_all)
    all_of(st2, s2_send, s2_recv).wait_recv()

    mean, var = merged(st2[...])
    sublane = lax.broadcasted_iota(jnp.int32, (8, 128), 0)
    wide = to_channels(jnp.where(sublane == 0, mean, lax.rsqrt(var + EPSILON)), member[...])
    mean_chan = wide[0:1]
    scale_chan = wide[1:2] * gain[...].reshape(1, CHANNELS)
    bias_chan = bias[...].reshape(1, CHANNELS)

    def normalised(block):
        return ((block.astype(F32) - mean_chan) * scale_chan + bias_chan).astype(BF16)

    own = normalised(xbuf[0])
    nbuf[0] = own
    forward(5, pairs_all)
    for kind, load in ((0, loads[2]), (1, loads[3])):
        load.wait()
        fresh = jnp.dot(own, (wk, wv)[kind][...], preferred_element_type=F32).astype(BF16)
        for pair in pairs_all:
            kv[middle, pair, kind] = fresh[:, pair * 128 : (pair + 1) * 128]
        result[1 + kind] = fresh
    loads[1].wait()
    for far in far_slots:
        for side in (0, 1):
            relay(side, far).wait_recv()

    @pl.loop(1, plane)
    def _(slot):
        nbuf[slot] = normalised(xbuf[slot])

    forward(6, range(0, 3))
    rows = plane * tokens
    normed = nbuf[...].reshape(rows, CHANNELS)
    for start in range(0, WIDTH, 256):
        end = min(start + 256, WIDTH)
        query = jnp.dot(normed, wq[:, start:end], preferred_element_type=F32).astype(BF16)
        query = query * jnp.asarray(HEAD_DIM**-0.5, BF16)
        for pair in range(start // 128, end // 128):
            at = pair * 128 - start
            qbuf[pair] = query[:, at : at + 128]
    forward(6, range(3, PAIRS))

    lane = lax.broadcasted_iota(jnp.int32, (1, 128), 1)
    low = lane < HEAD_DIM
    masks = (jnp.where(low, 1.0, 0.0).astype(BF16), jnp.where(low, 0.0, 1.0).astype(BF16))

    def gathered(kind, start, blocks, pair):
        return kv[start : start + blocks, pair, kind].reshape(blocks * tokens, 128)

    def scored(query, start, blocks, pair):
        both = jnp.concatenate([query * masks[0], query * masks[1]], axis=0)
        keys = gathered(0, start, blocks, pair)
        scores = lax.dot_general(both, keys, NT, preferred_element_type=F32)
        largest = jnp.max(scores, axis=-1, keepdims=True)
        return jnp.exp(scores - largest).astype(BF16), largest

    def valued(exps, largest, start, blocks, pair):
        ones = jnp.ones((blocks * tokens, 128), BF16)
        right = jnp.concatenate([gathered(1, start, blocks, pair), ones], axis=1)
        sums = jnp.dot(exps, right, preferred_element_type=F32)
        count = exps.shape[0] // 2

        def pick(tall):
            return jnp.where(low, tall[0:count], tall[count:])

        return pick(sums[:, 0:128]), pick(jnp.broadcast_to(largest, (2 * count, 128))), pick(sums[:, 128:])

    def attend(query_of, start, blocks, pairs, take):
        waiting = None
        for pair in list(pairs) + [None]:
            ready = waiting
            waiting = None if pair is None else (*scored(query_of(pair), start, blocks, pair), start, blocks, pair)
            if ready is not None:
                take(ready[-1], valued(*ready))

    def keep(pair, first, last, parts):
        for buf, value in zip((part_o, part_m, part_l), parts):
            buf[pair, first:last] = value

    def add_to(pair, parts):
        out, largest, total = parts
        old_largest = part_m[pair]
        top = jnp.maximum(largest, old_largest)
        now, before = jnp.exp(largest - top), jnp.exp(old_largest - top)
        return out * now + part_o[pair] * before, top, total * now + part_l[pair] * before

    need(0, half, pairs_all)
    attend(
        lambda pair: qbuf[pair, 0:tokens], 1, half, pairs_all,
        lambda pair, parts: keep(pair, 0, tokens, parts),
    )
    for pairs in (range(0, 3), range(3, PAIRS)):
        attend(
            lambda pair: qbuf[pair, tokens:rows], 0, half, pairs,
            lambda pair, parts: keep(pair, tokens, rows, parts),
        )
        forward(7, pairs)

    quarter = half // 2
    need(half, half + quarter, pairs_all)
    attend(
        lambda pair: qbuf[pair], half + 1, quarter, pairs_all,
        lambda pair, parts: keep(pair, 0, rows, add_to(pair, parts)),
    )

    def all_here(pair):
        need(half + quarter, depth, [pair])
        return qbuf[pair]

    def back(pair, slot):
        return remote(
            obuf.at[pair, slot], rbuf.at[pair, slot], o_send.at[pair], o_recv.at[pair],
            back_in_plane(slot),
        )

    def stat_back(slot):
        return remote(
            ostat_packed.at[slot], rstat_packed.at[slot], t_send, t_recv, back_in_plane(slot)
        )

    ostat[...] = jnp.zeros_like(ostat)
    within = lax.rem(lane, HEAD_DIM)

    def send_back(pair, parts):
        out, top, total = add_to(pair, parts)
        obuf[pair] = out.astype(BF16).reshape(plane, tokens, 128)
        for slot in range(1, plane):
            back(pair, slot).start()
        stats = jnp.where(within == pair, top, ostat[...])
        ostat[...] = jnp.where(within == pair + 8, total, stats)

    for pair in pairs_all:
        attend(all_here, half + 1 + quarter, quarter, [pair], send_back)

    packs = tokens // 8
    tiles = ostat[...].reshape(plane, packs, 8, 128)
    packed = sum(
        pltpu.roll(tiles[:, pack].reshape(plane * 8, 128), 16 * pack, 1) if pack else tiles[:, pack].reshape(plane * 8, 128)
        for pack in range(packs)
    )
    ostat_packed[...] = packed.reshape(plane, 8, 128)

    @pl.loop(1, plane)
    def _(slot):
        stat_back(slot).start()

    head_lane = lax.broadcasted_iota(jnp.int32, (128, WIDTH), 0)
    feature = lax.broadcasted_iota(jnp.int32, (128, WIDTH), 1)
    from_feature = lax.rem(head_lane, HEAD_DIM) * 128 + (head_lane // HEAD_DIM) * HEAD_DIM
    spread = jnp.where((feature >= from_feature) & (feature < from_feature + HEAD_DIM), 1.0, 0.0).astype(BF16)
    rstat_packed[0] = ostat_packed[0]

    all_of(st1, s1_send, s1_recv).wait_send()
    all_of(st2, s2_send, s2_recv).wait_send()
    every = kv.at[pl.ds(0, depth - 1)]
    remote(every, every, kv_send, kv_recv.at[0, 0], in_depth(1)).wait_send()
    all_of(xbuf, x_send, x_recv.at[0, 0]).wait_send()

    all_of(rstat_packed, t_send, t_recv).wait_recv()
    packed = rstat_packed[...].reshape(plane * 8, 128)
    tiles = [pltpu.roll(packed, 128 - 16 * pack, 1) if pack else packed for pack in range(packs)]
    stats = jnp.concatenate([tile.reshape(plane, 8, 128) for tile in tiles], axis=1)
    largest = jnp.max(stats, axis=0, keepdims=True)
    used = within < PAIRS
    weights = jnp.where(used, jnp.exp(stats - largest), 0.0)
    sums = pltpu.roll(stats.reshape(rows, 128), 120, 1).reshape(plane, tokens, 128)
    totals = jnp.where(used, jnp.sum(weights * sums, axis=0, keepdims=True), 1.0)
    shares = (weights / totals).reshape(rows, 128)
    upper = shares.astype(BF16)
    lower = (shares - upper.astype(F32)).astype(BF16)
    flat = jnp.dot(upper, spread, preferred_element_type=F32) + jnp.dot(lower, spread, preferred_element_type=F32)

    for pair in range(PAIRS):
        all_of(rbuf.at[pair], o_send.at[pair], o_recv.at[pair]).wait_recv()
        cols = slice(pair * 128, (pair + 1) * 128)
        scale = flat[:, cols].reshape(plane, tokens, 128)
        part = obuf[pair, 0].astype(F32) * scale[0]
        part = part + jnp.sum(rbuf[pair, 1:plane].astype(F32) * scale[1:], axis=0)
        result[0, :, cols] = part.astype(BF16)

    for pair in range(PAIRS):
        all_of(obuf.at[pair], o_send.at[pair], o_recv.at[pair]).wait_send()
    all_of(ostat_packed, t_send, t_recv).wait_send()


def hand_over(result, att, fresh_keys, fresh_values, sems):
    copies = [
        pltpu.make_async_copy(result.at[i], out, sems.at[i])
        for i, out in enumerate((att, fresh_keys, fresh_values))
    ]
    for copy in copies:
        copy.start()
    for copy in copies:
        copy.wait()


def on_device(plane, x, gain, bias, wq, wk, wv, k, v):
    depth = lax.axis_size("rows") // plane
    tokens = x.shape[0]
    rows = plane * tokens
    dma = pltpu.SemaphoreType.DMA
    anywhere = pl.BlockSpec(memory_space=pltpu.HBM)
    local = pl.BlockSpec(memory_space=pltpu.VMEM)
    out = jax.ShapeDtypeStruct((tokens, WIDTH), BF16)
    result = pl.pallas_call(
        functools.partial(kernel, depth, plane, tokens),
        out_shape=pltpu.VMEM((3, tokens, WIDTH), BF16),
        in_specs=[anywhere, local, local] + [anywhere] * 5,
        out_specs=local,
        scratch_shapes=[
            pltpu.VMEM((plane, tokens, CHANNELS), BF16),
            pltpu.VMEM((depth + 1, PAIRS, 2, tokens, 128), BF16),
            pltpu.VMEM((CHANNELS, WIDTH), BF16),
            pltpu.VMEM((CHANNELS, WIDTH), BF16),
            pltpu.VMEM((CHANNELS, WIDTH), BF16),
            pltpu.VMEM((CHANNELS, 128), BF16),
            pltpu.VMEM((plane, tokens, CHANNELS), BF16),
            pltpu.VMEM((PAIRS, rows, 128), BF16),
            pltpu.VMEM((plane, 2, 128), F32),
            pltpu.VMEM((depth, 2, 128), F32),
            pltpu.VMEM((PAIRS, rows, 128), F32),
            pltpu.VMEM((PAIRS, rows, 128), F32),
            pltpu.VMEM((PAIRS, rows, 128), F32),
            pltpu.VMEM((PAIRS, plane, tokens, 128), BF16),
            pltpu.VMEM((PAIRS, plane, tokens, 128), BF16),
            pltpu.VMEM((rows, 128), F32),
            pltpu.VMEM((plane, 8, 128), F32),
            pltpu.VMEM((plane, 8, 128), F32),
            dma((4,)), dma((PAIRS, 2)),
            dma, dma, dma, dma,
            dma, dma((plane, 2)),
            dma, dma((depth + 1, PAIRS)),
            dma((PAIRS,)), dma((PAIRS,)),
            dma, dma,
        ],
        compiler_params=pltpu.CompilerParams(
            collective_id=0, has_side_effects=True, vmem_limit_bytes=60 * 1024 * 1024
        ),
        name="attention_of_plane",
    )(x, gain, bias, wq, wk, wv, k, v)
    return pl.pallas_call(
        hand_over,
        out_shape=(out, out, out),
        in_specs=[local],
        out_specs=(anywhere,) * 3,
        scratch_shapes=[dma((3,))],
        name="hand_over",
    )(pltpu.with_memory_space_constraint(result, pltpu.VMEM))


def solution(mesh, plane=PLANE):
    split = P(("batch", "rows"), None)
    return jax.shard_map(
        functools.partial(on_device, plane),
        mesh=mesh,
        in_specs=(split, P(), P(), P(), P(), P(), split, split),
        out_specs=(split, split, split),
        check_vma=False,
    )
```

```python
import functools

import jax
import jax.numpy as jnp
from jax import lax
from jax.experimental import pallas as pl
from jax.experimental.pallas import tpu as pltpu
from jax.sharding import PartitionSpec as P

CHANNELS = 1280
GROUPS = 32
GROUP_WIDTH = CHANNELS // GROUPS
HEADS = 10
HEAD_DIM = 64
WIDTH = HEADS * HEAD_DIM
PAIRS = HEADS // 2
EPSILON = 1e-05
LINE = 4
BEFORE = (0, 0, 1, 0, 3, 4, 3, 6, 6)
PLANE = 8

F32 = jnp.float32
BF16 = jnp.bfloat16
MESH = pl.DeviceIdType.MESH
NT = (((1,), (1,)), ((), ()))


def exact_dot(value, right, dims):
    first = value.astype(BF16).astype(F32)
    second = (value - first).astype(BF16).astype(F32)
    terms = jnp.concatenate([first, second, value - first - second], axis=0).astype(BF16)
    out = lax.dot_general(terms, right, dims, preferred_element_type=F32)
    return out[0:8] + out[8:16] + out[16:24]


def to_groups(value, member):
    return exact_dot(value, member, (((1,), (0,)), ((), ())))


def to_channels(value, member):
    return exact_dot(value, member, NT)


def kernel(
    depth, plane, tokens,
    x_in, gain, bias, wq_in, wk_in, wv_in, k_in, v_in,
    result,
    xbuf, kv, wq, wk, wv, member, nbuf, qbuf, st1, st2,
    part_o, part_m, part_l, obuf, rbuf, ostat, ostat_packed, rstat_packed,
    in_sem, kv_sem, s1_send, s1_recv, s2_send, s2_recv, x_send, x_recv,
    kv_send, kv_recv, o_send, o_recv, t_send, t_recv,
):
    row = lax.axis_index("rows")
    z, p = row // plane, lax.rem(row, plane)
    half = depth // 2

    line = min(LINE, plane)

    def in_plane(step):
        x_to = lax.rem(p // line + step // line, plane // line)
        return {"rows": z * plane + x_to * line + lax.rem(lax.rem(p, line) + step % line, line)}

    def back_in_plane(step):
        return in_plane(step // line * line + lax.rem(line - step % line, line))

    def in_depth(step):
        return {"rows": lax.rem(z + step, depth) * plane + p}

    def remote(src, dst, send, recv, device):
        return pltpu.make_async_remote_copy(
            src_ref=src, dst_ref=dst, send_sem=send, recv_sem=recv,
            device_id=device, device_id_type=MESH,
        )

    barrier = pltpu.get_barrier_semaphore()

    @pl.loop(1, depth)
    def _(step):
        pl.semaphore_signal(barrier, inc=1, device_id=in_depth(step), device_id_type=MESH)

    @pl.loop(1, plane)
    def _(step):
        pl.semaphore_signal(barrier, inc=1, device_id=in_plane(step), device_id_type=MESH)

    blocks_in = [
        pltpu.make_async_copy(src.at[:, pl.ds(pair * 128, 128)], kv.at[0, pair, kind], kv_sem.at[pair, kind])
        for pair in range(PAIRS)
        for kind, src in enumerate((k_in, v_in))
    ]
    loads = [
        pltpu.make_async_copy(src, dst, in_sem.at[i])
        for i, (src, dst) in enumerate([(x_in, xbuf.at[0]), (wq_in, wq), (wk_in, wk), (wv_in, wv)])
    ]
    for load in blocks_in + loads:
        load.start()

    channel = lax.broadcasted_iota(jnp.int32, (CHANNELS, 128), 0)
    group = lax.broadcasted_iota(jnp.int32, (CHANNELS, 128), 1)
    first = group * GROUP_WIDTH
    inside = (channel >= first) & (channel < first + GROUP_WIDTH) & (group < GROUPS)
    member[...] = jnp.where(inside, 1.0, 0.0).astype(BF16)

    for load in blocks_in:
        load.wait()
    pl.semaphore_wait(barrier, plane + depth - 2)

    def stat1(step):
        return remote(st1.at[0], st1.at[step], s1_send, s1_recv, in_plane(step))

    def stat2(step):
        return remote(st2.at[0], st2.at[step], s2_send, s2_recv, in_depth(step))

    def share(step):
        return remote(xbuf.at[0], xbuf.at[step], x_send, x_recv.at[step, 0], in_plane(step))

    def relay(side, far):
        rows = pl.ds(side * (tokens // 2), tokens // 2)
        near = far - 1 if side == 0 else far + 1
        return remote(
            xbuf.at[near, rows], xbuf.at[far, rows], x_send, x_recv.at[far, side],
            in_plane(1 if side == 0 else line - 1),
        )

    slots = range(1, plane)
    far_slots = [step for step in slots if line == 4 and step % line == 2]
    near_slots = [step for step in slots if step not in far_slots]

    def all_of(buf, send, recv):
        rest = buf.at[pl.ds(1, buf.shape[0] - 1)]
        return remote(rest, rest, send, recv, in_plane(1))

    order = [0]
    for step in range(1, half):
        order += [step, depth - step]
    order += [half]
    middle = half
    place = {block: at if at < middle else at + 1 for at, block in enumerate(order)}

    def hop(way, pair, distance):
        before = BEFORE[distance]
        ends = [at if way == 0 else (depth - at) % depth for at in (before, distance)]
        by = distance - before if way == 0 else depth - (distance - before)
        here, there = place[ends[0]], place[ends[1]]
        return remote(kv.at[here, pair], kv.at[there, pair], kv_send, kv_recv.at[there, pair], in_depth(by))

    def length(way, pair):
        return half if pair % 2 == way else half - 1

    both_ways = (0, 1)
    pairs_all = range(PAIRS)
    seen = {(0, pair) for pair in pairs_all}

    def arrive(distance, pair):
        if (distance, pair) not in seen:
            seen.add((distance, pair))
            for way in both_ways:
                if distance <= length(way, pair):
                    hop(way, pair, distance).wait_recv()

    def need(first, last, pairs):
        for pair in pairs:
            for distance in sorted(min(block, depth - block) for block in order[first:last]):
                arrive(distance, pair)

    def forward(stop, pairs, ends=range(half, 0, -1)):
        for distance in ends:
            if BEFORE[distance] == stop:
                for pair in pairs:
                    arrive(stop, pair)
                    for way in both_ways:
                        if distance <= length(way, pair):
                            hop(way, pair, distance).start()

    def merged(stats):
        means, spread = stats[:, 0, :], stats[:, 1, :]
        mean = jnp.mean(means, axis=0, keepdims=True)
        apart = means - mean
        return mean, jnp.mean(spread + apart * apart, axis=0, keepdims=True)

    forward(0, pairs_all, (3,))
    loads[0].wait()
    for step in near_slots:
        share(step).start()

    x = xbuf[0]
    count = tokens * GROUP_WIDTH
    mean = jnp.sum(jnp.dot(x, member[...], preferred_element_type=F32), axis=0, keepdims=True) / count
    centered = x.astype(F32) - to_channels(jnp.broadcast_to(mean, (8, 128)), member[...])[0:1]
    squares = jnp.sum((centered * centered).reshape(tokens // 8, 8, CHANNELS), axis=0)
    var = jnp.sum(to_groups(squares, member[...]), axis=0, keepdims=True) / count
    st1[0, 0:1, :] = mean
    st1[0, 1:2, :] = var

    @pl.loop(1, plane)
    def _(step):
        stat1(step).start()

    forward(0, pairs_all, (1,))
    forward(3, range(0, 2))
    all_of(st1, s1_send, s1_recv).wait_recv()

    mean, var = merged(st1[...])
    st2[0, 0:1, :] = mean
    st2[0, 1:2, :] = var

    @pl.loop(1, depth)
    def _(step):
        stat2(step).start()

    forward(3, range(2, PAIRS))
    forward(1, pairs_all)
    for step in near_slots:
        share(step).wait_recv()
    for far in far_slots:
        for side in (0, 1):
            relay(side, far).start()
    forward(6, range(0, 2))
    all_of(st2, s2_send, s2_recv).wait_recv()

    mean, var = merged(st2[...])
    forward(6, range(2, PAIRS))
    sublane = lax.broadcasted_iota(jnp.int32, (8, 128), 0)
    wide = to_channels(jnp.where(sublane == 0, mean, lax.rsqrt(var + EPSILON)), member[...])
    mean_chan = wide[0:1]
    scale_chan = wide[1:2] * gain[...].reshape(1, CHANNELS)
    bias_chan = bias[...].reshape(1, CHANNELS)

    def normalised(block):
        return ((block.astype(F32) - mean_chan) * scale_chan + bias_chan).astype(BF16)

    own = normalised(xbuf[0])
    nbuf[0] = own
    for kind, load in ((0, loads[2]), (1, loads[3])):
        load.wait()
        fresh = jnp.dot(own, (wk, wv)[kind][...], preferred_element_type=F32).astype(BF16)
        for pair in pairs_all:
            kv[middle, pair, kind] = fresh[:, pair * 128 : (pair + 1) * 128]
        result[1 + kind] = fresh
    forward(4, pairs_all)
    loads[1].wait()
    for far in far_slots:
        for side in (0, 1):
            relay(side, far).wait_recv()

    @pl.loop(1, plane)
    def _(slot):
        nbuf[slot] = normalised(xbuf[slot])

    rows = plane * tokens
    normed = nbuf[...].reshape(rows, CHANNELS)
    for start in range(0, WIDTH, 256):
        end = min(start + 256, WIDTH)
        query = jnp.dot(normed, wq[:, start:end], preferred_element_type=F32).astype(BF16)
        query = query * jnp.asarray(HEAD_DIM**-0.5, BF16)
        for pair in range(start // 128, end // 128):
            at = pair * 128 - start
            qbuf[pair] = query[:, at : at + 128]

    lane = lax.broadcasted_iota(jnp.int32, (1, 128), 1)
    low = lane < HEAD_DIM
    masks = (jnp.where(low, 1.0, 0.0).astype(BF16), jnp.where(low, 0.0, 1.0).astype(BF16))

    def gathered(kind, start, blocks, pair):
        return kv[start : start + blocks, pair, kind].reshape(blocks * tokens, 128)

    def scored(query, start, blocks, pair):
        both = jnp.concatenate([query * masks[0], query * masks[1]], axis=0)
        keys = gathered(0, start, blocks, pair)
        scores = lax.dot_general(both, keys, NT, preferred_element_type=F32)
        largest = jnp.max(scores, axis=-1, keepdims=True)
        return jnp.exp(scores - largest).astype(BF16), largest

    def valued(exps, largest, start, blocks, pair):
        ones = jnp.ones((blocks * tokens, 128), BF16)
        right = jnp.concatenate([gathered(1, start, blocks, pair), ones], axis=1)
        sums = jnp.dot(exps, right, preferred_element_type=F32)
        count = exps.shape[0] // 2

        def pick(tall):
            return jnp.where(low, tall[0:count], tall[count:])

        return pick(sums[:, 0:128]), pick(jnp.broadcast_to(largest, (2 * count, 128))), pick(sums[:, 128:])

    def attend(query_of, start, blocks, pairs, take):
        waiting = None
        for pair in list(pairs) + [None]:
            ready = waiting
            waiting = None if pair is None else (*scored(query_of(pair), start, blocks, pair), start, blocks, pair)
            if ready is not None:
                take(ready[-1], valued(*ready))

    def keep(pair, first, last, parts):
        for buf, value in zip((part_o, part_m, part_l), parts):
            buf[pair, first:last] = value

    def add_to(pair, parts):
        out, largest, total = parts
        old_largest = part_m[pair]
        top = jnp.maximum(largest, old_largest)
        now, before = jnp.exp(largest - top), jnp.exp(old_largest - top)
        return out * now + part_o[pair] * before, top, total * now + part_l[pair] * before

    need(0, half, pairs_all)
    attend(
        lambda pair: qbuf[pair, 0:tokens], 1, half, pairs_all,
        lambda pair, parts: keep(pair, 0, tokens, parts),
    )
    attend(
        lambda pair: qbuf[pair, tokens:rows], 0, half, pairs_all,
        lambda pair, parts: keep(pair, tokens, rows, parts),
    )

    quarter = half // 2
    need(half, half + quarter, pairs_all)
    attend(
        lambda pair: qbuf[pair], half + 1, quarter, pairs_all,
        lambda pair, parts: keep(pair, 0, rows, add_to(pair, parts)),
    )

    def all_here(pair):
        need(half + quarter, depth, [pair])
        return qbuf[pair]

    def back(pair, slot):
        return remote(
            obuf.at[pair, slot], rbuf.at[pair, slot], o_send.at[pair], o_recv.at[pair],
            back_in_plane(slot),
        )

    def stat_back(slot):
        return remote(
            ostat_packed.at[slot], rstat_packed.at[slot], t_send, t_recv, back_in_plane(slot)
        )

    ostat[...] = jnp.zeros_like(ostat)
    within = lax.rem(lane, HEAD_DIM)

    def send_back(pair, parts):
        out, top, total = add_to(pair, parts)
        obuf[pair] = out.astype(BF16).reshape(plane, tokens, 128)
        for slot in range(1, plane):
            back(pair, slot).start()
        stats = jnp.where(within == pair, top, ostat[...])
        ostat[...] = jnp.where(within == pair + 8, total, stats)

    attend(all_here, half + 1 + quarter, quarter, pairs_all, send_back)

    packs = tokens // 8
    tiles = ostat[...].reshape(plane, packs, 8, 128)
    packed = sum(
        pltpu.roll(tiles[:, pack].reshape(plane * 8, 128), 16 * pack, 1) if pack else tiles[:, pack].reshape(plane * 8, 128)
        for pack in range(packs)
    )
    ostat_packed[...] = packed.reshape(plane, 8, 128)

    @pl.loop(1, plane)
    def _(slot):
        stat_back(slot).start()

    head_lane = lax.broadcasted_iota(jnp.int32, (128, WIDTH), 0)
    feature = lax.broadcasted_iota(jnp.int32, (128, WIDTH), 1)
    from_feature = lax.rem(head_lane, HEAD_DIM) * 128 + (head_lane // HEAD_DIM) * HEAD_DIM
    spread = jnp.where((feature >= from_feature) & (feature < from_feature + HEAD_DIM), 1.0, 0.0).astype(BF16)
    rstat_packed[0] = ostat_packed[0]

    all_of(st1, s1_send, s1_recv).wait_send()
    all_of(st2, s2_send, s2_recv).wait_send()
    every = kv.at[pl.ds(0, depth - 1)]
    remote(every, every, kv_send, kv_recv.at[0, 0], in_depth(1)).wait_send()
    all_of(xbuf, x_send, x_recv.at[0, 0]).wait_send()

    all_of(rstat_packed, t_send, t_recv).wait_recv()
    packed = rstat_packed[...].reshape(plane * 8, 128)
    tiles = [pltpu.roll(packed, 128 - 16 * pack, 1) if pack else packed for pack in range(packs)]
    stats = jnp.concatenate([tile.reshape(plane, 8, 128) for tile in tiles], axis=1)
    largest = jnp.max(stats, axis=0, keepdims=True)
    used = within < PAIRS
    weights = jnp.where(used, jnp.exp(stats - largest), 0.0)
    sums = pltpu.roll(stats.reshape(rows, 128), 120, 1).reshape(plane, tokens, 128)
    totals = jnp.where(used, jnp.sum(weights * sums, axis=0, keepdims=True), 1.0)
    shares = (weights / totals).reshape(rows, 128)
    upper = shares.astype(BF16)
    lower = (shares - upper.astype(F32)).astype(BF16)
    flat = jnp.dot(upper, spread, preferred_element_type=F32) + jnp.dot(lower, spread, preferred_element_type=F32)

    for pair in range(PAIRS):
        all_of(rbuf.at[pair], o_send.at[pair], o_recv.at[pair]).wait_recv()
        cols = slice(pair * 128, (pair + 1) * 128)
        scale = flat[:, cols].reshape(plane, tokens, 128)
        part = obuf[pair, 0].astype(F32) * scale[0]
        part = part + jnp.sum(rbuf[pair, 1:plane].astype(F32) * scale[1:], axis=0)
        result[0, :, cols] = part.astype(BF16)

    for pair in range(PAIRS):
        all_of(obuf.at[pair], o_send.at[pair], o_recv.at[pair]).wait_send()
    all_of(ostat_packed, t_send, t_recv).wait_send()


def hand_over(result, att, fresh_keys, fresh_values, sems):
    copies = [
        pltpu.make_async_copy(result.at[i], out, sems.at[i])
        for i, out in enumerate((att, fresh_keys, fresh_values))
    ]
    for copy in copies:
        copy.start()
    for copy in copies:
        copy.wait()


def on_device(plane, x, gain, bias, wq, wk, wv, k, v):
    depth = lax.axis_size("rows") // plane
    tokens = x.shape[0]
    rows = plane * tokens
    dma = pltpu.SemaphoreType.DMA
    anywhere = pl.BlockSpec(memory_space=pltpu.HBM)
    local = pl.BlockSpec(memory_space=pltpu.VMEM)
    out = jax.ShapeDtypeStruct((tokens, WIDTH), BF16)
    result = pl.pallas_call(
        functools.partial(kernel, depth, plane, tokens),
        out_shape=pltpu.VMEM((3, tokens, WIDTH), BF16),
        in_specs=[anywhere, local, local] + [anywhere] * 5,
        out_specs=local,
        scratch_shapes=[
            pltpu.VMEM((plane, tokens, CHANNELS), BF16),
            pltpu.VMEM((depth + 1, PAIRS, 2, tokens, 128), BF16),
            pltpu.VMEM((CHANNELS, WIDTH), BF16),
            pltpu.VMEM((CHANNELS, WIDTH), BF16),
            pltpu.VMEM((CHANNELS, WIDTH), BF16),
            pltpu.VMEM((CHANNELS, 128), BF16),
            pltpu.VMEM((plane, tokens, CHANNELS), BF16),
            pltpu.VMEM((PAIRS, rows, 128), BF16),
            pltpu.VMEM((plane, 2, 128), F32),
            pltpu.VMEM((depth, 2, 128), F32),
            pltpu.VMEM((PAIRS, rows, 128), F32),
            pltpu.VMEM((PAIRS, rows, 128), F32),
            pltpu.VMEM((PAIRS, rows, 128), F32),
            pltpu.VMEM((PAIRS, plane, tokens, 128), BF16),
            pltpu.VMEM((PAIRS, plane, tokens, 128), BF16),
            pltpu.VMEM((rows, 128), F32),
            pltpu.VMEM((plane, 8, 128), F32),
            pltpu.VMEM((plane, 8, 128), F32),
            dma((4,)), dma((PAIRS, 2)),
            dma, dma, dma, dma,
            dma, dma((plane, 2)),
            dma, dma((depth + 1, PAIRS)),
            dma((PAIRS,)), dma((PAIRS,)),
            dma, dma,
        ],
        compiler_params=pltpu.CompilerParams(
            collective_id=0, has_side_effects=True, vmem_limit_bytes=60 * 1024 * 1024
        ),
        name="attention_of_plane",
    )(x, gain, bias, wq, wk, wv, k, v)
    return pl.pallas_call(
        hand_over,
        out_shape=(out, out, out),
        in_specs=[local],
        out_specs=(anywhere,) * 3,
        scratch_shapes=[dma((3,))],
        name="hand_over",
    )(pltpu.with_memory_space_constraint(result, pltpu.VMEM))


def solution(mesh, plane=PLANE):
    split = P(("batch", "rows"), None)
    return jax.shard_map(
        functools.partial(on_device, plane),
        mesh=mesh,
        in_specs=(split, P(), P(), P(), P(), P(), split, split),
        out_specs=(split, split, split),
        check_vma=False,
    )
```

```python
import functools

import jax
import jax.numpy as jnp
from jax import lax
from jax.experimental import pallas as pl
from jax.experimental.pallas import tpu as pltpu
from jax.sharding import PartitionSpec as P

CHANNELS = 1280
GROUPS = 32
GROUP_WIDTH = CHANNELS // GROUPS
HEADS = 10
HEAD_DIM = 64
WIDTH = HEADS * HEAD_DIM
PAIRS = HEADS // 2
EPSILON = 1e-05
LINE = 4
PLANE = 8

F32 = jnp.float32
BF16 = jnp.bfloat16
MESH = pl.DeviceIdType.MESH
NT = (((1,), (1,)), ((), ()))


def exact_dot(value, right, dims):
    first = value.astype(BF16).astype(F32)
    second = (value - first).astype(BF16).astype(F32)
    terms = jnp.concatenate([first, second, value - first - second], axis=0).astype(BF16)
    out = lax.dot_general(terms, right, dims, preferred_element_type=F32)
    return out[0:8] + out[8:16] + out[16:24]


def to_groups(value, member):
    return exact_dot(value, member, (((1,), (0,)), ((), ())))


def to_channels(value, member):
    return exact_dot(value, member, NT)


def kernel(
    depth, plane, tokens,
    x_in, gain, bias, wq_in, wk_in, wv_in, k_in, v_in,
    result,
    xbuf, kv, wq, wk, wv, member, nbuf, qbuf, st1, st2,
    part_o, part_m, part_l, obuf, rbuf, ostat, ostat_packed, rstat_packed,
    in_sem, kv_sem, s1_send, s1_recv, s2_send, s2_recv, x_send, x_recv,
    kv_send, kv_recv, o_send, o_recv, t_send, t_recv,
):
    row = lax.axis_index("rows")
    z, p = row // plane, lax.rem(row, plane)
    half = depth // 2

    line = min(LINE, plane)

    def in_plane(step):
        x_to = lax.rem(p // line + step // line, plane // line)
        return {"rows": z * plane + x_to * line + lax.rem(lax.rem(p, line) + step % line, line)}

    def back_in_plane(step):
        return in_plane(step // line * line + lax.rem(line - step % line, line))

    def in_depth(step):
        return {"rows": lax.rem(z + step, depth) * plane + p}

    def remote(src, dst, send, recv, device):
        return pltpu.make_async_remote_copy(
            src_ref=src, dst_ref=dst, send_sem=send, recv_sem=recv,
            device_id=device, device_id_type=MESH,
        )

    barrier = pltpu.get_barrier_semaphore()

    @pl.loop(1, depth)
    def _(step):
        pl.semaphore_signal(barrier, inc=1, device_id=in_depth(step), device_id_type=MESH)

    @pl.loop(1, plane)
    def _(step):
        pl.semaphore_signal(barrier, inc=1, device_id=in_plane(step), device_id_type=MESH)

    blocks_in = [
        pltpu.make_async_copy(src.at[:, pl.ds(pair * 128, 128)], kv.at[0, pair, kind], kv_sem.at[pair, kind])
        for pair in range(PAIRS)
        for kind, src in enumerate((k_in, v_in))
    ]
    loads = [
        pltpu.make_async_copy(src, dst, in_sem.at[i])
        for i, (src, dst) in enumerate([(x_in, xbuf.at[0]), (wq_in, wq), (wk_in, wk), (wv_in, wv)])
    ]
    for load in blocks_in + loads:
        load.start()

    channel = lax.broadcasted_iota(jnp.int32, (CHANNELS, 128), 0)
    group = lax.broadcasted_iota(jnp.int32, (CHANNELS, 128), 1)
    first = group * GROUP_WIDTH
    inside = (channel >= first) & (channel < first + GROUP_WIDTH) & (group < GROUPS)
    member[...] = jnp.where(inside, 1.0, 0.0).astype(BF16)

    for load in blocks_in:
        load.wait()
    pl.semaphore_wait(barrier, plane + depth - 2)

    def stat1(step):
        return remote(st1.at[0], st1.at[step], s1_send, s1_recv, in_plane(step))

    def stat2(step):
        return remote(st2.at[0], st2.at[step], s2_send, s2_recv, in_depth(step))

    def share(step):
        return remote(xbuf.at[0], xbuf.at[step], x_send, x_recv.at[step, 0], in_plane(step))

    def relay(side, far):
        rows = pl.ds(side * (tokens // 2), tokens // 2)
        near = far - 1 if side == 0 else far + 1
        return remote(
            xbuf.at[near, rows], xbuf.at[far, rows], x_send, x_recv.at[far, side],
            in_plane(1 if side == 0 else line - 1),
        )

    slots = range(1, plane)
    far_slots = [step for step in slots if line == 4 and step % line == 2]
    near_slots = [step for step in slots if step not in far_slots]

    def all_of(buf, send, recv):
        rest = buf.at[pl.ds(1, buf.shape[0] - 1)]
        return remote(rest, rest, send, recv, in_plane(1))

    order = [0]
    for step in range(1, half):
        order += [step, depth - step]
    order += [half]
    middle = half
    place = {block: at if at < middle else at + 1 for at, block in enumerate(order)}

    def hop(way, pair, distance):
        before = distance - 1 if distance % 2 else distance - 2
        ends = [at if way == 0 else (depth - at) % depth for at in (before, distance)]
        by = distance - before if way == 0 else depth - (distance - before)
        here, there = place[ends[0]], place[ends[1]]
        return remote(kv.at[here, pair], kv.at[there, pair], kv_send, kv_recv.at[there, pair], in_depth(by))

    def length(way, pair):
        return half if pair % 2 == way else half - 1

    both_ways = (0, 1)
    pairs_all = range(PAIRS)
    seen = {(0, pair) for pair in pairs_all}

    def arrive(distance, pair):
        if (distance, pair) not in seen:
            seen.add((distance, pair))
            for way in both_ways:
                if distance <= length(way, pair):
                    hop(way, pair, distance).wait_recv()

    def need(first, last, pairs):
        for pair in pairs:
            for distance in sorted(min(block, depth - block) for block in order[first:last]):
                arrive(distance, pair)

    def forward(stop, pairs, hops=(2, 1)):
        if stop >= half:
            return
        for by in hops:
            for pair in pairs:
                arrive(stop, pair)
                for way in both_ways:
                    if stop + by <= length(way, pair):
                        hop(way, pair, stop + by).start()

    def merged(stats):
        means, spread = stats[:, 0, :], stats[:, 1, :]
        mean = jnp.mean(means, axis=0, keepdims=True)
        apart = means - mean
        return mean, jnp.mean(spread + apart * apart, axis=0, keepdims=True)

    forward(0, pairs_all, (2,))
    loads[0].wait()
    for step in near_slots:
        share(step).start()

    x = xbuf[0]
    count = tokens * GROUP_WIDTH
    mean = jnp.sum(jnp.dot(x, member[...], preferred_element_type=F32), axis=0, keepdims=True) / count
    centered = x.astype(F32) - to_channels(jnp.broadcast_to(mean, (8, 128)), member[...])[0:1]
    squares = jnp.sum((centered * centered).reshape(tokens // 8, 8, CHANNELS), axis=0)
    var = jnp.sum(to_groups(squares, member[...]), axis=0, keepdims=True) / count
    st1[0, 0:1, :] = mean
    st1[0, 1:2, :] = var

    @pl.loop(1, plane)
    def _(step):
        stat1(step).start()

    forward(0, pairs_all, (1,))
    forward(2, range(0, 2))
    all_of(st1, s1_send, s1_recv).wait_recv()

    mean, var = merged(st1[...])
    st2[0, 0:1, :] = mean
    st2[0, 1:2, :] = var

    @pl.loop(1, depth)
    def _(step):
        stat2(step).start()

    forward(2, range(2, PAIRS))
    for step in near_slots:
        share(step).wait_recv()
    for far in far_slots:
        for side in (0, 1):
            relay(side, far).start()
    forward(4, range(0, 3))
    all_of(st2, s2_send, s2_recv).wait_recv()

    mean, var = merged(st2[...])
    forward(4, range(3, PAIRS))
    sublane = lax.broadcasted_iota(jnp.int32, (8, 128), 0)
    wide = to_channels(jnp.where(sublane == 0, mean, lax.rsqrt(var + EPSILON)), member[...])
    mean_chan = wide[0:1]
    scale_chan = wide[1:2] * gain[...].reshape(1, CHANNELS)
    bias_chan = bias[...].reshape(1, CHANNELS)

    def normalised(block):
        return ((block.astype(F32) - mean_chan) * scale_chan + bias_chan).astype(BF16)

    own = normalised(xbuf[0])
    nbuf[0] = own
    for kind, load in ((0, loads[2]), (1, loads[3])):
        load.wait()
        fresh = jnp.dot(own, (wk, wv)[kind][...], preferred_element_type=F32).astype(BF16)
        for pair in pairs_all:
            kv[middle, pair, kind] = fresh[:, pair * 128 : (pair + 1) * 128]
        result[1 + kind] = fresh
    forward(6, range(0, 3))
    loads[1].wait()
    for far in far_slots:
        for side in (0, 1):
            relay(side, far).wait_recv()

    @pl.loop(1, plane)
    def _(slot):
        nbuf[slot] = normalised(xbuf[slot])

    rows = plane * tokens
    normed = nbuf[...].reshape(rows, CHANNELS)
    for start in range(0, WIDTH, 256):
        end = min(start + 256, WIDTH)
        query = jnp.dot(normed, wq[:, start:end], preferred_element_type=F32).astype(BF16)
        query = query * jnp.asarray(HEAD_DIM**-0.5, BF16)
        for pair in range(start // 128, end // 128):
            at = pair * 128 - start
            qbuf[pair] = query[:, at : at + 128]
    forward(6, range(3, PAIRS))

    lane = lax.broadcasted_iota(jnp.int32, (1, 128), 1)
    low = lane < HEAD_DIM
    masks = (jnp.where(low, 1.0, 0.0).astype(BF16), jnp.where(low, 0.0, 1.0).astype(BF16))

    def gathered(kind, start, blocks, pair):
        return kv[start : start + blocks, pair, kind].reshape(blocks * tokens, 128)

    def scored(query, start, blocks, pair):
        both = jnp.concatenate([query * masks[0], query * masks[1]], axis=0)
        keys = gathered(0, start, blocks, pair)
        scores = lax.dot_general(both, keys, NT, preferred_element_type=F32)
        largest = jnp.max(scores, axis=-1, keepdims=True)
        return jnp.exp(scores - largest).astype(BF16), largest

    def valued(exps, largest, start, blocks, pair):
        ones = jnp.ones((blocks * tokens, 128), BF16)
        right = jnp.concatenate([gathered(1, start, blocks, pair), ones], axis=1)
        sums = jnp.dot(exps, right, preferred_element_type=F32)
        count = exps.shape[0] // 2

        def pick(tall):
            return jnp.where(low, tall[0:count], tall[count:])

        return pick(sums[:, 0:128]), pick(jnp.broadcast_to(largest, (2 * count, 128))), pick(sums[:, 128:])

    def attend(query_of, start, blocks, pairs, take):
        waiting = None
        for pair in list(pairs) + [None]:
            ready = waiting
            waiting = None if pair is None else (*scored(query_of(pair), start, blocks, pair), start, blocks, pair)
            if ready is not None:
                take(ready[-1], valued(*ready))

    def keep(pair, first, last, parts):
        for buf, value in zip((part_o, part_m, part_l), parts):
            buf[pair, first:last] = value

    def add_to(pair, parts):
        out, largest, total = parts
        old_largest = part_m[pair]
        top = jnp.maximum(largest, old_largest)
        now, before = jnp.exp(largest - top), jnp.exp(old_largest - top)
        return out * now + part_o[pair] * before, top, total * now + part_l[pair] * before

    need(0, half, pairs_all)
    attend(
        lambda pair: qbuf[pair, 0:tokens], 1, half, pairs_all,
        lambda pair, parts: keep(pair, 0, tokens, parts),
    )
    attend(
        lambda pair: qbuf[pair, tokens:rows], 0, half, pairs_all,
        lambda pair, parts: keep(pair, tokens, rows, parts),
    )

    quarter = half // 2
    need(half, half + quarter, pairs_all)
    attend(
        lambda pair: qbuf[pair], half + 1, quarter, pairs_all,
        lambda pair, parts: keep(pair, 0, rows, add_to(pair, parts)),
    )

    def all_here(pair):
        need(half + quarter, depth, [pair])
        return qbuf[pair]

    def back(pair, slot):
        return remote(
            obuf.at[pair, slot], rbuf.at[pair, slot], o_send.at[pair], o_recv.at[pair],
            back_in_plane(slot),
        )

    def stat_back(slot):
        return remote(
            ostat_packed.at[slot], rstat_packed.at[slot], t_send, t_recv, back_in_plane(slot)
        )

    ostat[...] = jnp.zeros_like(ostat)
    within = lax.rem(lane, HEAD_DIM)

    def send_back(pair, parts):
        out, top, total = add_to(pair, parts)
        obuf[pair] = out.astype(BF16).reshape(plane, tokens, 128)
        for slot in range(1, plane):
            back(pair, slot).start()
        stats = jnp.where(within == pair, top, ostat[...])
        ostat[...] = jnp.where(within == pair + 8, total, stats)

    for pair in pairs_all:
        attend(all_here, half + 1 + quarter, quarter, [pair], send_back)

    packs = tokens // 8
    tiles = ostat[...].reshape(plane, packs, 8, 128)
    packed = sum(
        pltpu.roll(tiles[:, pack].reshape(plane * 8, 128), 16 * pack, 1) if pack else tiles[:, pack].reshape(plane * 8, 128)
        for pack in range(packs)
    )
    ostat_packed[...] = packed.reshape(plane, 8, 128)

    @pl.loop(1, plane)
    def _(slot):
        stat_back(slot).start()

    head_lane = lax.broadcasted_iota(jnp.int32, (128, WIDTH), 0)
    feature = lax.broadcasted_iota(jnp.int32, (128, WIDTH), 1)
    from_feature = lax.rem(head_lane, HEAD_DIM) * 128 + (head_lane // HEAD_DIM) * HEAD_DIM
    spread = jnp.where((feature >= from_feature) & (feature < from_feature + HEAD_DIM), 1.0, 0.0).astype(BF16)
    rstat_packed[0] = ostat_packed[0]

    all_of(st1, s1_send, s1_recv).wait_send()
    all_of(st2, s2_send, s2_recv).wait_send()
    every = kv.at[pl.ds(0, depth - 1)]
    remote(every, every, kv_send, kv_recv.at[0, 0], in_depth(1)).wait_send()
    all_of(xbuf, x_send, x_recv.at[0, 0]).wait_send()

    all_of(rstat_packed, t_send, t_recv).wait_recv()
    packed = rstat_packed[...].reshape(plane * 8, 128)
    tiles = [pltpu.roll(packed, 128 - 16 * pack, 1) if pack else packed for pack in range(packs)]
    stats = jnp.concatenate([tile.reshape(plane, 8, 128) for tile in tiles], axis=1)
    largest = jnp.max(stats, axis=0, keepdims=True)
    used = within < PAIRS
    weights = jnp.where(used, jnp.exp(stats - largest), 0.0)
    sums = pltpu.roll(stats.reshape(rows, 128), 120, 1).reshape(plane, tokens, 128)
    totals = jnp.where(used, jnp.sum(weights * sums, axis=0, keepdims=True), 1.0)
    shares = (weights / totals).reshape(rows, 128)
    upper = shares.astype(BF16)
    lower = (shares - upper.astype(F32)).astype(BF16)
    flat = jnp.dot(upper, spread, preferred_element_type=F32) + jnp.dot(lower, spread, preferred_element_type=F32)

    for pair in range(PAIRS):
        all_of(rbuf.at[pair], o_send.at[pair], o_recv.at[pair]).wait_recv()
        cols = slice(pair * 128, (pair + 1) * 128)
        scale = flat[:, cols].reshape(plane, tokens, 128)
        part = obuf[pair, 0].astype(F32) * scale[0]
        part = part + jnp.sum(rbuf[pair, 1:plane].astype(F32) * scale[1:], axis=0)
        result[0, :, cols] = part.astype(BF16)

    for pair in range(PAIRS):
        all_of(obuf.at[pair], o_send.at[pair], o_recv.at[pair]).wait_send()
    all_of(ostat_packed, t_send, t_recv).wait_send()


def hand_over(result, att, fresh_keys, fresh_values, sems):
    copies = [
        pltpu.make_async_copy(result.at[i], out, sems.at[i])
        for i, out in enumerate((att, fresh_keys, fresh_values))
    ]
    for copy in copies:
        copy.start()
    for copy in copies:
        copy.wait()


def on_device(plane, x, gain, bias, wq, wk, wv, k, v):
    depth = lax.axis_size("rows") // plane
    tokens = x.shape[0]
    rows = plane * tokens
    dma = pltpu.SemaphoreType.DMA
    anywhere = pl.BlockSpec(memory_space=pltpu.HBM)
    local = pl.BlockSpec(memory_space=pltpu.VMEM)
    out = jax.ShapeDtypeStruct((tokens, WIDTH), BF16)
    result = pl.pallas_call(
        functools.partial(kernel, depth, plane, tokens),
        out_shape=pltpu.VMEM((3, tokens, WIDTH), BF16),
        in_specs=[anywhere, local, local] + [anywhere] * 5,
        out_specs=local,
        scratch_shapes=[
            pltpu.VMEM((plane, tokens, CHANNELS), BF16),
            pltpu.VMEM((depth + 1, PAIRS, 2, tokens, 128), BF16),
            pltpu.VMEM((CHANNELS, WIDTH), BF16),
            pltpu.VMEM((CHANNELS, WIDTH), BF16),
            pltpu.VMEM((CHANNELS, WIDTH), BF16),
            pltpu.VMEM((CHANNELS, 128), BF16),
            pltpu.VMEM((plane, tokens, CHANNELS), BF16),
            pltpu.VMEM((PAIRS, rows, 128), BF16),
            pltpu.VMEM((plane, 2, 128), F32),
            pltpu.VMEM((depth, 2, 128), F32),
            pltpu.VMEM((PAIRS, rows, 128), F32),
            pltpu.VMEM((PAIRS, rows, 128), F32),
            pltpu.VMEM((PAIRS, rows, 128), F32),
            pltpu.VMEM((PAIRS, plane, tokens, 128), BF16),
            pltpu.VMEM((PAIRS, plane, tokens, 128), BF16),
            pltpu.VMEM((rows, 128), F32),
            pltpu.VMEM((plane, 8, 128), F32),
            pltpu.VMEM((plane, 8, 128), F32),
            dma((4,)), dma((PAIRS, 2)),
            dma, dma, dma, dma,
            dma, dma((plane, 2)),
            dma, dma((depth + 1, PAIRS)),
            dma((PAIRS,)), dma((PAIRS,)),
            dma, dma,
        ],
        compiler_params=pltpu.CompilerParams(
            collective_id=0, has_side_effects=True, vmem_limit_bytes=60 * 1024 * 1024
        ),
        name="attention_of_plane",
    )(x, gain, bias, wq, wk, wv, k, v)
    return pl.pallas_call(
        hand_over,
        out_shape=(out, out, out),
        in_specs=[local],
        out_specs=(anywhere,) * 3,
        scratch_shapes=[dma((3,))],
        name="hand_over",
    )(pltpu.with_memory_space_constraint(result, pltpu.VMEM))


def solution(mesh, plane=PLANE):
    split = P(("batch", "rows"), None)
    return jax.shard_map(
        functools.partial(on_device, plane),
        mesh=mesh,
        in_specs=(split, P(), P(), P(), P(), P(), split, split),
        out_specs=(split, split, split),
        check_vma=False,
    )
```
